32 devices in a mesh: row: 4 (over x, core), col: 2 (over y), layer: 4 (over z).
Axes of the slice: x: 2, y: 2, z: 4, core: 2. Of those that a mesh axis runs over, the one named last changes fastest.
Arguments:
- a_vals: bfloat16 [4, 2, 4, 32, 4096], P('row', 'col', 'layer'), may hold values from -6 to 6
- a_rows: int32 [4, 2, 4, 32], P('row', 'col', 'layer'), may hold values from 0 to 7, as said below
- a_cols: int32 [4, 2, 4, 32], P('row', 'col', 'layer'), may hold values from 0 to 15, as said below
- a_count: int32 [4, 2, 4], P('row', 'col', 'layer'), may hold values from 8 to 32, as said below
- p_vals: bfloat16 [4, 2, 4, 32, 4096], P('row', 'col', 'layer'), may hold values from -0.1875 to 0.1875
- p_rows: int32 [4, 2, 4, 32], P('row', 'col', 'layer'), may hold values from 0 to 7, as said below
- p_cols: int32 [4, 2, 4, 32], P('row', 'col', 'layer'), may hold values from 0 to 7, as said below
- p_count: int32 [4, 2, 4], P('row', 'col', 'layer'), may hold values from 16 to 32, as said below
Outputs:
- galerkin: float32 [2048, 1024], P('row', ('col', 'layer'))
The draws below stay inside these ranges and needn't reach their ends.
Inputs may be any that keep to these rules, and one draw needn't show every extreme that they name: Within one tile the slots name distinct blocks; a_rows indexes the 8 block rows of the tile. a_cols indexes the 16 inner block columns of the tile. Slots from a_count on are unused; some tile uses all 32 slots and some the fewest. Within one tile the slots name distinct blocks; p_rows indexes the 8 inner block rows of the tile. p_cols indexes the 8 coarse block columns of the tile. Slots from p_count on are unused; some tile uses all 32 slots and some the fewest.
All inputs are finite; a program needn't handle non-finite values.
Results may differ from the reference program's by a relative error of at most 0.0003.
Values may be sent and summed in bfloat16 or wider, within the bound.
A program may use at most 128 MiB of HBM per device.

```python
import jax
import jax.numpy as jnp
from jax import lax

GRID_ROWS = 4
GRID_COLS = 2
LAYERS = 4
BS = 64
RB = 8
KB = 16
JB = 8
PBLK = 32
ABLK = 32
N_ROW = 4
N_COL = 2
N_LAYER = 4


def slot_position_table(key, position_count, slots_total):
    tiles = N_ROW * N_COL * N_LAYER
    random_keys = jax.random.split(key, tiles)
    chosen_slots = jax.vmap(lambda inner_index: jax.random.permutation(inner_index, position_count)[:slots_total])(random_keys)
    return chosen_slots.reshape(N_ROW, N_COL, N_LAYER, slots_total).astype(jnp.int32)


def tile_counts(key, lowest, highest, cubic):
    tiles = N_ROW * N_COL * N_LAYER
    first, second, third = jax.random.split(key, 3)
    if cubic:
        raw = jax.random.randint(first, (tiles,), 1, highest + 1)
        counts = jnp.maximum(lowest, raw * raw * raw // (highest * highest))
    else:
        counts = jax.random.randint(first, (tiles,), lowest, highest + 1)
    top = jax.random.randint(second, (), 0, tiles)
    bottom = (top + 1 + jax.random.randint(third, (), 0, tiles - 1)) % tiles
    index = jnp.arange(tiles)
    counts = jnp.where(index == top, highest, counts)
    counts = jnp.where(index == bottom, lowest, counts)
    return counts.reshape(N_ROW, N_COL, N_LAYER).astype(jnp.int32)


def draw_a_rows(key, part):
    return slot_position_table(jax.random.fold_in(key, 101), RB * KB, ABLK) // KB


def draw_a_cols(key, part):
    return slot_position_table(jax.random.fold_in(key, 101), RB * KB, ABLK) % KB


def draw_a_count(key, part):
    return tile_counts(jax.random.fold_in(key, 103), max(1, ABLK // 4), ABLK, True)


def draw_p_rows(key, part):
    return slot_position_table(jax.random.fold_in(key, 107), N_COL * KB // N_ROW * JB, PBLK) // JB


def draw_p_cols(key, part):
    return slot_position_table(jax.random.fold_in(key, 107), N_COL * KB // N_ROW * JB, PBLK) % JB


def draw_p_count(key, part):
    return tile_counts(jax.random.fold_in(key, 109), PBLK // 2, PBLK, False)


def steps_of(own_key, dims, shards, low, top_value):
    def one(axis_at, blocks):
        steps = jax.random.uniform(jax.random.fold_in(jax.random.fold_in(own_key, 6), axis_at), (blocks,), jnp.float32, low / len(shards), top_value / len(shards))
        return jnp.repeat(jnp.exp(steps), dims[axis_at] // blocks).reshape((-1,) + (1,) * (len(dims) - axis_at - 1))

    level = one(*shards[0])
    for cut in shards[1:]:
        level = level * one(*cut)
    return level


def centred(rng, dims, deviation, limit, shards=(), held_as=jnp.bfloat16):
    loudness = steps_of(rng, dims, shards, -0.22, 0.18) if shards else 1.0
    drawn = jax.random.normal(rng, dims, jnp.float32) * deviation * loudness
    return jnp.minimum(jnp.maximum(drawn, -limit), limit).astype(held_as)


def setup_inputs(seed: int = 0) -> dict:
    arg_keys = jax.random.split(jax.random.key(seed), 9)
    a_vals = centred(arg_keys[0], (GRID_ROWS, GRID_COLS, LAYERS, ABLK, BS * BS), 1.0, 6.0, ((0, 4), (1, 2), (2, 4)))
    a_rows = draw_a_rows(jax.random.fold_in(arg_keys[8], 71), 0)
    a_cols = draw_a_cols(jax.random.fold_in(arg_keys[8], 71), 0)
    a_count = draw_a_count(jax.random.fold_in(arg_keys[8], 71), 0)
    p_vals = centred(arg_keys[4], (GRID_ROWS, GRID_COLS, LAYERS, PBLK, BS * BS), 1024 ** -0.5, 0.1875, ((0, 4), (1, 2), (2, 4)))
    p_rows = draw_p_rows(jax.random.fold_in(arg_keys[8], 71), 0)
    p_cols = draw_p_cols(jax.random.fold_in(arg_keys[8], 71), 0)
    p_count = draw_p_count(jax.random.fold_in(arg_keys[8], 71), 0)
    return dict(a_vals=a_vals, a_rows=a_rows, a_cols=a_cols, a_count=a_count, p_vals=p_vals, p_rows=p_rows, p_cols=p_cols, p_count=p_count)


def densify_tile(values, block_row_count, block_cols, filled, row_blocks, col_blocks, width):
    slot_count = values.shape[0]
    position = block_row_count * col_blocks + block_cols
    active = jnp.arange(slot_count, dtype=jnp.int32) < filled
    target = jnp.arange(row_blocks * col_blocks, dtype=jnp.int32)
    onehot = ((target[:, None] == position[None, :]) & active[None, :]).astype(jnp.float32)
    dense_flat = jnp.dot(onehot, values.astype(jnp.float32), precision=lax.Precision.HIGHEST).astype(jnp.bfloat16)
    shaped = dense_flat.reshape(row_blocks, col_blocks, width, width).transpose(0, 2, 1, 3)
    return shaped.reshape(row_blocks * width, col_blocks * width)


def reference(a_vals, a_rows, a_cols, a_count, p_vals, p_rows, p_cols, p_count):
    kb_rows = N_COL * KB // N_ROW
    coarse_wide = N_COL * JB * BS

    def expand(values, block_row_count, block_cols, filled):
        return densify_tile(values, block_row_count, block_cols, filled, kb_rows, JB, BS)

    dense_p = jax.vmap(jax.vmap(jax.vmap(expand)))(p_vals, p_rows, p_cols, p_count)
    layered = dense_p.transpose(2, 0, 3, 1, 4).reshape(N_LAYER, N_ROW * kb_rows, BS, coarse_wide)
    col_index = jnp.repeat(jnp.arange(N_COL, dtype=jnp.int32), N_LAYER)
    layer_index = jnp.tile(jnp.arange(N_LAYER, dtype=jnp.int32), N_COL)

    def slab(inputs):
        values, block_row_count, block_cols, filled = inputs
        values = values.reshape(N_COL * N_LAYER, ABLK, BS * BS)
        block_row_count = block_row_count.reshape(N_COL * N_LAYER, ABLK)
        block_cols = block_cols.reshape(N_COL * N_LAYER, ABLK)
        filled = filled.reshape(N_COL * N_LAYER)

        def step(running, tile):
            tile_vals, tile_rows, tile_cols, tile_fill, which_col, which_layer = tile
            blocks = tile_vals.reshape(ABLK, BS, BS).astype(jnp.float32)
            source = lax.dynamic_index_in_dim(layered, which_layer, 0, keepdims=False)
            chosen_slots = jnp.take(source, which_col * KB + tile_cols, axis=0).astype(jnp.float32)
            products = jnp.einsum("sab,sbc->sac", blocks, chosen_slots, precision=lax.Precision.HIGHEST)
            active = jnp.arange(ABLK, dtype=jnp.int32) < tile_fill
            segment = jnp.where(active, tile_rows, RB).astype(jnp.int32)
            summed = jax.ops.segment_sum(products, segment, num_segments=RB + 1)[:RB]
            return running + summed, None

        start_value = jnp.zeros((RB, BS, coarse_wide), jnp.float32)
        total, _ = lax.scan(step, start_value, (values, block_row_count, block_cols, filled, col_index, layer_index))
        return total.reshape(RB * BS, coarse_wide)

    result = lax.map(slab, (a_vals, a_rows, a_cols, a_count))
    return result.reshape(N_ROW * RB * BS, coarse_wide)
```

```python
import functools

import jax
import jax.numpy as jnp
from jax import lax
from jax.experimental import pallas as pl
from jax.experimental.pallas import tpu as pltpu
from jax.sharding import PartitionSpec as P

BS = 64
RB = 8
KB = 16
JB = 8
LANES = 128
HALF = BS * BS // 2
MESH = pl.DeviceIdType.MESH
F32 = jnp.float32
BF16 = jnp.bfloat16


def positions(rows, cols, count, width):
    slot = lax.broadcasted_iota(jnp.int32, rows.shape, 1)
    pos = jnp.where(slot < count, rows * width + cols, -1)
    row = jnp.concatenate([pos] * (LANES // pos.shape[1]), axis=1)
    return jnp.broadcast_to(row, (8, LANES))


def pair_onehot(pos, pairs, width, slots):
    shape = (pairs * 8, 2 * slots)
    row = lax.broadcasted_iota(jnp.int32, shape, 0)
    lane = lax.broadcasted_iota(jnp.int32, shape, 1)
    want = (row % 8) * width + 2 * (row // 8) + lane // slots
    return jnp.where(want == pos[0:1, : 2 * slots], 1.0, 0.0).astype(BF16)


def spread(vals, onehot, pairs, store, first=0, last=8):
    slots = vals.shape[0]
    low = lax.broadcasted_iota(jnp.int32, (slots, LANES), 1) < BS

    def body(step, carry):
        v = vals[:, pl.ds(pl.multiple_of(step * 512, 512), 512)].astype(F32)
        parts = []
        for g in range(4):
            a = v[:, g * LANES : (g + 1) * LANES]
            b = pltpu.roll(a, BS, 1)
            parts.append(jnp.concatenate([jnp.where(low, a, 0.0), jnp.where(low, 0.0, b)], axis=0))
            parts.append(jnp.concatenate([jnp.where(low, b, 0.0), jnp.where(low, 0.0, a)], axis=0))
        w = jnp.concatenate(parts, axis=1).astype(BF16)
        d = jnp.dot(onehot, w, preferred_element_type=F32)
        for p in range(pairs):
            rows = [d[p * 8 : (p + 1) * 8, i * LANES : (i + 1) * LANES] for i in range(8)]
            store(step, p, jnp.concatenate(rows, axis=0).astype(BF16))
        return carry

    lax.fori_loop(first, last, body, 0, unroll=True)


def quad_onehot(pos, slots):
    row = lax.broadcasted_iota(jnp.int32, (64, slots), 0)
    want = (row % 8) * JB + ((row // 8) % 2) * 4 + row // 16
    return jnp.where(want == pos[0:1, :slots], 1.0, 0.0).astype(BF16)


def lane_of(shape):
    return lax.broadcasted_iota(jnp.int32, shape, 1)


def four(lane, parts):
    low = jnp.where(lane < 32, parts[0], parts[1])
    high = jnp.where(lane < 96, parts[2], parts[3])
    return jnp.where(lane < 64, low, high)


def split(src, dst):
    slots = src.shape[0]
    first = lane_of((slots, LANES)) % BS < 32
    for t in range(16):
        a = src[:, 256 * t : 256 * t + LANES].astype(F32)
        b = src[:, 256 * t + LANES : 256 * t + 256].astype(F32)
        at = slice(t * LANES, (t + 1) * LANES)
        dst[0, :, at] = jnp.where(first, a, pltpu.roll(b, 32, 1)).astype(BF16)
        dst[1, :, at] = jnp.where(first, pltpu.roll(a, 96, 1), b).astype(BF16)


def spread_half(vals, onehot, store):
    lane = lane_of((8, LANES))
    for step in range(4):
        v = vals[:, step * 512 : (step + 1) * 512].astype(F32)
        parts = []
        for g in range(4):
            a = v[:, g * LANES : (g + 1) * LANES]
            parts += [a] + [pltpu.roll(a, 32 * r, 1) for r in range(1, 4)]
        w = jnp.concatenate(parts, axis=1).astype(BF16)
        d = jnp.dot(onehot, w, preferred_element_type=F32)
        for z in range(2):
            rows = []
            for kin in range(16):
                g, u = kin // 4, (0, 2, 1, 3)[kin % 4]
                at = [(g * 4 + (m - u) % 4) * LANES for m in range(4)]
                rows.append(
                    four(lane, [d[m * 16 + z * 8 : m * 16 + z * 8 + 8, at[m] : at[m] + LANES] for m in range(4)])
                )
            store(step, z, jnp.concatenate(rows, axis=0).astype(BF16))


def kernel(
    n_row, n_col, n_layer, a_hbm, p_hbm, *rest,
):
    small_hbm, out, small, scratch = rest[:6], rest[6], rest[7:13], rest[13:]
    (
    a_buf, p_raw, p_buf, a_pos, p_pos, a_own_pos, p_own_pos, a_dense, a_mixed, p_dense, order, acc, total,
    code, code_in, peak, peak_in,
    loc_sem, a_send, a_recv, ap_send, ap_recv, p_send, p_recv, r_send, r_recv, s_send, s_recv, pp_send, pp_recv,
    c_send, c_recv, m_send, m_recv,
    ) = scratch
    row, col, lay = lax.axis_index("row"), lax.axis_index("col"), lax.axis_index("layer")
    core = lax.rem(row, 2)
    sib = row + 1 - 2 * core
    chips = n_row // 2
    slots = a_hbm.shape[0]

    barrier = pltpu.get_barrier_semaphore()
    for d in range(1, n_row):
        pl.semaphore_signal(barrier, inc=1, device_id={"row": lax.rem(row + d, n_row)}, device_id_type=MESH)
    for d in range(1, n_col):
        pl.semaphore_signal(barrier, inc=1, device_id={"col": lax.rem(col + d, n_col)}, device_id_type=MESH)
    for d in range(1, n_layer):
        pl.semaphore_signal(barrier, inc=1, device_id={"layer": lax.rem(lay + d, n_layer)}, device_id_type=MESH)
    own_a = pltpu.make_async_copy(a_hbm, a_buf.at[0], loc_sem.at[0])
    own_p = pltpu.make_async_copy(p_hbm, p_raw, loc_sem.at[1])
    tables = [pltpu.make_async_copy(small_hbm[k], small[k], loc_sem.at[2 + k]) for k in range(6)]
    own_p.start()
    for copy in tables:
        copy.start()
    own_a.start()

    def remote(src, dst, send, recv, where):
        return pltpu.make_async_remote_copy(
            src_ref=src, dst_ref=dst, send_sem=send, recv_sem=recv, device_id=where, device_id_type=MESH
        )

    def piece(ref, h):
        return ref.at[:, pl.ds(h * HALF, HALF)]

    across, relay, over, over_marks, marks = {}, {}, {}, {}, []
    for h in range(2):
        for d in range(1, chips):
            to = {"row": lax.rem(row + 2 * d, n_row)}
            across[d, h] = remote(p_buf.at[0, h], p_buf.at[2 * d, h], p_send.at[d, h], p_recv.at[d, h], to)
            relay[d, h] = remote(
                p_buf.at[2 * d, h], p_buf.at[2 * d + 1, h], r_send.at[d, h], r_recv.at[d, h], {"row": sib}
            )
        for d in range(1, n_col):
            to = {"col": lax.rem(col + d, n_col)}
            over[d, h] = remote(piece(a_hbm, h), piece(a_buf.at[d], h), a_send.at[d, h], a_recv.at[d, h], to)
    for d in range(1, n_col):
        to = {"col": lax.rem(col + d, n_col)}
        over_marks[d] = remote(a_own_pos, a_pos.at[d], ap_send.at[d], ap_recv.at[d], to)
    for d in range(1, n_row):
        to = lax.rem(row + d, n_row) if d % 2 == 0 else lax.rem(sib + d - 1, n_row)
        marks.append(remote(p_own_pos, p_pos.at[d], pp_send.at[d], pp_recv.at[d], {"row": to}))
    beside = remote(p_buf.at[0], p_buf.at[1], s_send, s_recv, {"row": sib})

    own_p.wait()
    split(p_raw, p_buf.at[0])
    for copy in tables:
        copy.wait()
    a_rows, a_cols, a_count, p_rows, p_cols, p_count = small
    a_own_pos[...] = positions(a_rows[...], a_cols[...], a_count[...], KB)
    p_own_pos[...] = positions(p_rows[...], p_cols[...], p_count[...], JB)
    pl.semaphore_wait(barrier, n_row + n_col + n_layer - 3)
    for h in range(2):
        for d in range(1, chips):
            across[d, h].start()
        for d in range(1, n_col):
            over[d, h].start()
        if h == 0:
            for copy in marks + list(over_marks.values()) + [beside]:
                copy.start()

    shape = order.shape
    r = lax.broadcasted_iota(jnp.int32, shape, 0)
    c = lax.broadcasted_iota(jnp.int32, shape, 1)
    order[...] = jnp.where(c == (r % BS) * 8 + r // BS, 1.0, 0.0).astype(BF16)

    def take_a(d, h):
        pos = a_own_pos if d == 0 else a_pos.at[d]
        onehot = pair_onehot(pos[...], KB // 2, KB, slots)
        first = 2 * lax.rem(col - d + n_col, n_col)

        def store(step, p, rows):
            lanes = pl.ds((p % 4) * LANES, LANES)
            a_mixed[p // 4, pl.ds(pl.multiple_of(step * 64, 64), 64), lanes] = rows

        spread(a_buf.at[d], onehot, KB // 2, store, 4 * h, 4 * h + 4)
        rows = pl.ds(h * 256, 256)
        for q in range(2):
            a_dense[first + q, rows, :] = jnp.dot(
                a_mixed[q, rows, :], order[...], preferred_element_type=F32
            ).astype(BF16)

    def take_p(d, h):
        pos = p_own_pos if d == 0 else p_pos.at[d]

        def store(step, z, rows):
            p_dense[h, d, step * LANES : (step + 1) * LANES, z * LANES : (z + 1) * LANES] = rows

        spread_half(p_buf.at[d, h], quad_onehot(pos[...], slots), store)

    def source(d):
        base = row if d % 2 == 0 else sib
        return lax.rem(base - 2 * (d // 2) + n_row, n_row)

    inner = jnp.logical_or(lay == 1, lay == 2)
    near = lay + 1 - 2 * lax.rem(lay, 2)
    far = lax.rem(lay + 2, 4)
    opposite = 3 - lay
    lane = lane_of((LANES, LANES))

    def multiply(rh, ch):
        rows = pl.ds(rh * 256, 256)
        k = 2 * ch + rh
        sum_ = jnp.dot(a_dense[source(0), rows, :], p_dense[ch, 0], preferred_element_type=F32)
        for d in range(1, n_row):
            sum_ += jnp.dot(a_dense[source(d), rows, :], p_dense[ch, d], preferred_element_type=F32)
        acc[k] = sum_

    def packed(k, to):
        lanes = pl.ds(pl.multiple_of((to // 2) * LANES, LANES), LANES)
        x, y = acc[k, 0:LANES, lanes], acc[k, LANES : 2 * LANES, lanes]
        odd = lax.rem(to, 2)
        stays = jnp.where(odd == 0, x, y)
        moves = pltpu.roll(jnp.where(odd == 0, y, x), BS, 1)
        return jnp.where(lane // BS == odd, stays, moves)

    def encode(k, j, x):
        top = jnp.maximum(jnp.max(jnp.abs(x), axis=0, keepdims=True), 1.2e-38)
        peak[k, j] = top
        q = jnp.round((x * (1.0 / top)) * 32767.0)
        code[k, j] = q.astype(jnp.int32).astype(jnp.int16)

    def decode(k, j):
        q = code_in[k, j].astype(jnp.int32).astype(F32)
        return (q * (1.0 / 32767.0)) * peak_in[k, j]

    def hand(k, j, slot, to):
        where = {"layer": to}
        return (
            remote(code.at[k, j], code_in.at[k, slot], c_send.at[k, j], c_recv.at[k, slot], where),
            remote(peak.at[k, j], peak_in.at[k, slot], m_send.at[k, j], m_recv.at[k, slot], where),
        )

    def via(k):
        return hand(k, 0, jnp.where(inner, 3, 0), jnp.where(inner, opposite, near))

    def start(copies):
        for copy in copies:
            copy.start()

    def arrive(copies):
        for copy in copies:
            copy.wait_recv()

    def launch(k):
        encode(k, 0, packed(k, opposite))
        start(via(k))

        @pl.when(jnp.logical_not(inner))
        def _():
            encode(k, 2, packed(k, far))
            start(hand(k, 2, 2, far))

        encode(k, 1, packed(k, near))
        start(hand(k, 1, 1, near))
        total[k] = packed(k, lay)

    def forward(k):
        @pl.when(inner)
        def _():
            arrive(hand(k, 0, 0, near))
            encode(k, 2, packed(k, far) + decode(k, 0))
            start(hand(k, 2, 2, far))

    def collect(k):
        @pl.when(inner)
        def _():
            arrive(hand(k, 0, 3, opposite))
            total[k] += decode(k, 3)

        arrive(hand(k, 1, 1, near))
        x = total[k] + decode(k, 1)
        arrive(hand(k, 2, 2, far))
        return x + decode(k, 2)

    take_p(0, 0)
    own_a.wait()
    take_a(0, 0)
    beside.wait_recv()
    marks[0].wait_recv()
    take_p(1, 0)
    take_a(0, 1)
    take_p(0, 1)
    take_p(1, 1)
    for d in range(1, chips):
        across[d, 0].wait_recv()
        relay[d, 0].start()
    for d in range(1, n_col):
        over_marks[d].wait_recv()
        over[d, 0].wait_recv()
        take_a(d, 0)
    for d in range(2, n_row):
        marks[d - 1].wait_recv()
        if d % 2:
            relay[d // 2, 0].wait_recv()
        take_p(d, 0)
    multiply(0, 0)
    launch(0)
    for d in range(1, chips):
        across[d, 1].wait_recv()
        relay[d, 1].start()
    for d in range(1, n_col):
        over[d, 1].wait_recv()
        take_a(d, 1)
    multiply(1, 0)
    launch(1)
    forward(0)
    for d in range(2, n_row):
        if d % 2:
            relay[d // 2, 1].wait_recv()
        take_p(d, 1)
    multiply(0, 1)
    launch(2)
    multiply(1, 1)
    launch(3)
    for k in range(1, 4):
        forward(k)
    for rh in range(2):
        f, g = collect(rh), collect(2 + rh)
        for s in range(2):
            if s == 0:
                x = four(lane, [f, pltpu.roll(g, 32, 1), pltpu.roll(f, 32, 1), pltpu.roll(g, 64, 1)])
            else:
                x = four(lane, [pltpu.roll(f, 64, 1), pltpu.roll(g, 96, 1), pltpu.roll(f, 96, 1), g])
            out[pl.ds(rh * 32 + s * 16, 16)] = x.reshape(16, 8, LANES)

    sums = []
    for k in range(4):
        sums += list(via(k)) + list(hand(k, 2, 2, far)) + list(hand(k, 1, 1, near))
    for copy in list(across.values()) + list(relay.values()) + list(over.values()) + list(over_marks.values()):
        copy.wait_send()
    for copy in marks + sums + [beside]:
        copy.wait_send()


def solution(mesh):
    n_row, n_col, n_layer = (mesh.shape[k] for k in ("row", "col", "layer"))

    def on_device(a_vals, a_rows, a_cols, a_count, p_vals, p_rows, p_cols, p_count):
        slots = a_vals.shape[3]
        wide = BS * BS
        any_space = pl.BlockSpec(memory_space=pltpu.HBM)
        vmem = pl.BlockSpec(memory_space=pltpu.VMEM)
        dma = pltpu.SemaphoreType.DMA
        chips = n_row // 2
        got = pl.pallas_call(
            functools.partial(kernel, n_row, n_col, n_layer),
            out_shape=jax.ShapeDtypeStruct((BS, RB, LANES), F32),
            in_specs=[any_space] * 8,
            out_specs=vmem,
            scratch_shapes=(
                [pltpu.VMEM((1, slots), jnp.int32)] * 2 + [pltpu.VMEM((1, 1), jnp.int32)]
            ) * 2 + [
                pltpu.VMEM((n_col, slots, wide), BF16),
                pltpu.VMEM((slots, wide), BF16),
                pltpu.VMEM((n_row, 2, slots, HALF), BF16),
                pltpu.VMEM((n_col, 8, LANES), jnp.int32),
                pltpu.VMEM((n_row, 8, LANES), jnp.int32),
                pltpu.VMEM((8, LANES), jnp.int32),
                pltpu.VMEM((8, LANES), jnp.int32),
                pltpu.VMEM((n_row, RB * BS, 8 * BS), BF16),
                pltpu.VMEM((2, RB * BS, 8 * BS), BF16),
                pltpu.VMEM((2, n_row, 8 * BS, JB * BS // 2), BF16),
                pltpu.VMEM((8 * BS, 8 * BS), BF16),
                pltpu.VMEM((4, 256, 256), F32),
                pltpu.VMEM((4, LANES, LANES), F32),
                pltpu.VMEM((4, 3, LANES, LANES), jnp.int16),
                pltpu.VMEM((4, 4, LANES, LANES), jnp.int16),
                pltpu.VMEM((4, 3, 1, LANES), F32),
                pltpu.VMEM((4, 4, 1, LANES), F32),
                dma((8,)),
                dma((n_col, 2)), dma((n_col, 2)), dma((n_col,)), dma((n_col,)),
                dma((chips, 2)), dma((chips, 2)), dma((chips, 2)), dma((chips, 2)),
                dma, dma,
                dma((n_row,)), dma((n_row,)),
                dma((4, 3)), dma((4, 4)), dma((4, 3)), dma((4, 4)),
            ],
            compiler_params=pltpu.CompilerParams(
                collective_id=0, has_side_effects=True, vmem_limit_bytes=56_200_000
            ),
        )(
            a_vals.reshape(slots, wide), p_vals.reshape(slots, wide),
            a_rows.reshape(1, slots), a_cols.reshape(1, slots), a_count.reshape(1, 1),
            p_rows.reshape(1, slots), p_cols.reshape(1, slots), p_count.reshape(1, 1),
        )
        return got.transpose(1, 0, 2).reshape(RB * BS, LANES)

    placed = (
        P("row", "col", "layer", None, None),
        P("row", "col", "layer", None),
        P("row", "col", "layer", None),
        P("row", "col", "layer"),
    ) * 2
    return jax.shard_map(
        on_device, mesh=mesh, in_specs=placed, out_specs=P("row", ("col", "layer")), check_vma=False
    )
```

```python
import functools

import jax
import jax.numpy as jnp
from jax import lax
from jax.experimental import pallas as pl
from jax.experimental.pallas import tpu as pltpu
from jax.sharding import PartitionSpec as P

BS = 64
RB = 8
KB = 16
JB = 8
LANES = 128
MESH = pl.DeviceIdType.MESH
F32 = jnp.float32
BF16 = jnp.bfloat16


def positions(rows, cols, count, width):
    slot = lax.broadcasted_iota(jnp.int32, rows.shape, 1)
    pos = jnp.where(slot < count, rows * width + cols, -1)
    row = jnp.concatenate([pos] * (LANES // pos.shape[1]), axis=1)
    return jnp.broadcast_to(row, (8, LANES))


def pair_onehot(pos, pairs, width, slots):
    shape = (pairs * 8, 2 * slots)
    row = lax.broadcasted_iota(jnp.int32, shape, 0)
    lane = lax.broadcasted_iota(jnp.int32, shape, 1)
    want = (row % 8) * width + 2 * (row // 8) + lane // slots
    return jnp.where(want == pos[0:1, : 2 * slots], 1.0, 0.0).astype(BF16)


def spread(vals, onehot, pairs, store, first=0, last=8):
    slots = vals.shape[0]
    low = lax.broadcasted_iota(jnp.int32, (slots, LANES), 1) < BS

    def body(step, carry):
        v = vals[:, pl.ds(pl.multiple_of(step * 512, 512), 512)].astype(F32)
        parts = []
        for g in range(4):
            a = v[:, g * LANES : (g + 1) * LANES]
            b = pltpu.roll(a, BS, 1)
            parts.append(jnp.concatenate([jnp.where(low, a, 0.0), jnp.where(low, 0.0, b)], axis=0))
            parts.append(jnp.concatenate([jnp.where(low, b, 0.0), jnp.where(low, 0.0, a)], axis=0))
        w = jnp.concatenate(parts, axis=1).astype(BF16)
        d = jnp.dot(onehot, w, preferred_element_type=F32)
        for p in range(pairs):
            rows = [d[p * 8 : (p + 1) * 8, i * LANES : (i + 1) * LANES] for i in range(8)]
            store(step, p, jnp.concatenate(rows, axis=0).astype(BF16))
        return carry

    lax.fori_loop(first, last, body, 0, unroll=True)


def kernel(
    n_row, n_col, n_layer, a_hbm, p_hbm, *rest,
):
    small_hbm, (a_count, p_count), out, small, scratch = rest[:4], rest[4:6], rest[6], rest[7:11], rest[11:]
    (
    a_buf, p_buf, a_pos, p_pos, a_own_pos, p_own_pos, a_dense, a_mixed, p_dense, order, acc, code, code_in, peak, peak_in,
    loc_sem, a_send, a_recv, ap_send, ap_recv, p_send, p_recv, r_send, r_recv, s_send, s_recv, pp_send, pp_recv,
    c_send, c_recv, m_send, m_recv,
    ) = scratch
    row, col, lay = lax.axis_index("row"), lax.axis_index("col"), lax.axis_index("layer")
    core = lax.rem(row, 2)
    sib = row + 1 - 2 * core
    chips = n_row // 2
    half = BS * BS // 2
    slots = a_hbm.shape[0]

    own_a = pltpu.make_async_copy(a_hbm, a_buf.at[0], loc_sem.at[0])
    own_p = pltpu.make_async_copy(p_hbm, p_buf.at[0], loc_sem.at[1])
    tables = [pltpu.make_async_copy(small_hbm[k], small[k], loc_sem.at[2 + k]) for k in range(4)]
    for copy in tables:
        copy.start()
    own_p.start()
    own_a.start()
    barrier = pltpu.get_barrier_semaphore()
    for d in range(1, n_row):
        pl.semaphore_signal(barrier, inc=1, device_id={"row": lax.rem(row + d, n_row)}, device_id_type=MESH)
    for d in range(1, n_col):
        pl.semaphore_signal(barrier, inc=1, device_id={"col": lax.rem(col + d, n_col)}, device_id_type=MESH)
    for d in range(1, n_layer):
        pl.semaphore_signal(barrier, inc=1, device_id={"layer": lax.rem(lay + d, n_layer)}, device_id_type=MESH)
    pl.semaphore_wait(barrier, n_row + n_col + n_layer - 3)

    def remote(src, dst, send, recv, where):
        return pltpu.make_async_remote_copy(
            src_ref=src, dst_ref=dst, send_sem=send, recv_sem=recv, device_id=where, device_id_type=MESH
        )

    def piece(ref, h):
        return ref.at[:, pl.ds(h * half, half)]

    across, relay = {}, {}
    for h in range(2):
        for d in range(1, chips):
            to = lax.rem(row + 2 * d, n_row)
            across[d, h] = remote(
                piece(p_hbm, h), piece(p_buf.at[2 * d], h), p_send.at[d, h], p_recv.at[d, h], {"row": to}
            )
            relay[d, h] = remote(
                piece(p_buf.at[2 * d], h), piece(p_buf.at[2 * d + 1], h), r_send.at[d, h], r_recv.at[d, h], {"row": sib}
            )
            if h == 0:
                across[d, h].start()
    over = {}
    for d in range(1, n_col):
        to = {"col": lax.rem(col + d, n_col)}
        for h in range(2):
            over[d, h] = remote(piece(a_hbm, h), piece(a_buf.at[d], h), a_send.at[d, h], a_recv.at[d, h], to)
            if h == 0:
                over[d, h].start()
    for copy in tables:
        copy.wait()
    a_rows, a_cols, p_rows, p_cols = small
    a_own_pos[...] = positions(a_rows[...], a_cols[...], a_count[0, 0], KB)
    p_own_pos[...] = positions(p_rows[...], p_cols[...], p_count[0, 0], JB)
    over_marks = {}
    for d in range(1, n_col):
        to = {"col": lax.rem(col + d, n_col)}
        over_marks[d] = remote(a_own_pos, a_pos.at[d], ap_send.at[d], ap_recv.at[d], to)
        over_marks[d].start()
    marks = []
    for d in range(1, n_row):
        if d % 2 == 0:
            to = lax.rem(row + d, n_row)
        else:
            to = lax.rem(sib + d - 1, n_row)
        marks.append(remote(p_own_pos, p_pos.at[d], pp_send.at[d], pp_recv.at[d], {"row": to}))
        marks[-1].start()
    beside = remote(p_hbm, p_buf.at[1], s_send, s_recv, {"row": sib})
    beside.start()
    for d in range(1, chips):
        across[d, 1].start()
    for d in range(1, n_col):
        over[d, 1].start()

    shape = order.shape
    r = lax.broadcasted_iota(jnp.int32, shape, 0)
    c = lax.broadcasted_iota(jnp.int32, shape, 1)
    order[...] = jnp.where(c == (r % BS) * 8 + r // BS, 1.0, 0.0).astype(BF16)

    def take_a(d, h):
        pos = a_own_pos if d == 0 else a_pos.at[d]
        onehot = pair_onehot(pos[...], KB // 2, KB, slots)
        first = 2 * lax.rem(col - d + n_col, n_col)

        def store(step, p, rows):
            lanes = pl.ds((p % 4) * LANES, LANES)
            a_mixed[p // 4, pl.ds(pl.multiple_of(step * 64, 64), 64), lanes] = rows

        spread(a_buf.at[d], onehot, KB // 2, store, 4 * h, 4 * h + 4)
        rows = pl.ds(h * 256, 256)
        for q in range(2):
            a_dense[first + q, rows, :] = jnp.dot(
                a_mixed[q, rows, :], order[...], preferred_element_type=F32
            ).astype(BF16)

    def take_p(d, h):
        pos = p_own_pos if d == 0 else p_pos.at[d]
        onehot = pair_onehot(pos[...], JB // 2, JB, slots)

        def store(step, p, rows):
            p_dense[d, pl.ds(pl.multiple_of(step * 64, 64), 64), p * LANES : (p + 1) * LANES] = rows

        spread(p_buf.at[d], onehot, JB // 2, store, 4 * h, 4 * h + 4)

    def source(d):
        base = row if d % 2 == 0 else sib
        return lax.rem(base - 2 * (d // 2) + n_row, n_row)

    own_p.wait()
    take_p(0, 0)
    take_p(0, 1)
    own_a.wait()
    take_a(0, 0)
    take_a(0, 1)
    beside.wait_recv()
    marks[0].wait_recv()
    take_p(1, 0)
    take_p(1, 1)
    for h in range(2):
        for d in range(1, chips):
            across[d, h].wait_recv()
            relay[d, h].start()
        for d in range(1, n_col):
            if h == 0:
                over_marks[d].wait_recv()
            over[d, h].wait_recv()
            take_a(d, h)
        rows = pl.ds(h * 256, 256)
        acc[rows, :] = jnp.dot(a_dense[source(0), rows, :], p_dense[0], preferred_element_type=F32) + jnp.dot(
            a_dense[source(1), rows, :], p_dense[1], preferred_element_type=F32
        )
        if h == 0:
            for d in range(2, n_row):
                marks[d - 1].wait_recv()
                if d % 2:
                    relay[d // 2, 0].wait_recv()
                take_p(d, 0)
    for d in range(2, n_row):
        if d % 2:
            relay[d // 2, 1].wait_recv()
        take_p(d, 1)
        acc[...] += jnp.dot(a_dense[source(d)], p_dense[d], preferred_element_type=F32)

    def mine(to):
        return acc[:, pl.ds(pl.multiple_of(to * LANES, LANES), LANES)].reshape(BS, 8, LANES)

    def encode(k, x):
        top = jnp.maximum(jnp.max(jnp.abs(x), axis=0), 1.2e-38)
        peak[k] = top
        q = jnp.round((x * (1.0 / top)) * 32767.0)
        code[k] = q.astype(jnp.int32).astype(jnp.int16).reshape(BS * 8, LANES)

    def decode(k):
        q = code_in[k].astype(jnp.int32).astype(F32).reshape(BS, 8, LANES)
        return (q * (1.0 / 32767.0)) * peak_in[k]

    def hand(k, slot, to):
        where = {"layer": to}
        return (
            remote(code.at[k], code_in.at[slot], c_send.at[k], c_recv.at[slot], where),
            remote(peak.at[k], peak_in.at[slot], m_send.at[k], m_recv.at[slot], where),
        )

    def start(copies):
        for copy in copies:
            copy.start()

    def arrive(copies):
        for copy in copies:
            copy.wait_recv()

    sums = []
    if n_layer == 4:
        inner = jnp.logical_or(lay == 1, lay == 2)
        near = lay + 1 - 2 * lax.rem(lay, 2)
        far = lax.rem(lay + 2, 4)
        across_to = 3 - lay
        via = hand(0, jnp.where(inner, 3, 0), jnp.where(inner, across_to, near))
        by_far, by_near = hand(2, 2, far), hand(1, 1, near)
        taken = hand(0, 0, near)
        third = hand(0, 3, across_to)
        sums = list(via) + list(by_far) + list(by_near)

        encode(0, mine(across_to))
        start(via)

        @pl.when(jnp.logical_not(inner))
        def _():
            encode(2, mine(far))
            start(by_far)

        encode(1, mine(near))
        start(by_near)

        @pl.when(inner)
        def _():
            arrive(taken)
            encode(2, mine(far) + decode(0))
            start(by_far)
            arrive(third)
            out[...] = mine(lay) + decode(3)

        @pl.when(jnp.logical_not(inner))
        def _():
            out[...] = mine(lay)

        arrive(by_near)
        total = out[...] + decode(1)
        arrive(by_far)
        total = total + decode(2)
    else:
        for d in range(n_layer - 1, 0, -1):
            to = lax.rem(lay + d, n_layer)
            encode(d, mine(to))
            copies = hand(d, d, to)
            start(copies)
            sums.extend(copies)
        total = mine(lay)
        for d in range(n_layer - 1, 0, -1):
            arrive(hand(d, d, lax.rem(lay + d, n_layer)))
            total = total + decode(d)
    out[...] = total

    for h in range(2):
        for d in range(1, chips):
            across[d, h].wait_send()
            relay[d, h].wait_send()
    for copy in list(over.values()) + list(over_marks.values()) + marks + sums + [beside]:
        copy.wait_send()


def solution(mesh):
    n_row, n_col, n_layer = (mesh.shape[k] for k in ("row", "col", "layer"))

    def on_device(a_vals, a_rows, a_cols, a_count, p_vals, p_rows, p_cols, p_count):
        slots = a_vals.shape[3]
        wide = BS * BS
        any_space = pl.BlockSpec(memory_space=pltpu.HBM)
        vmem = pl.BlockSpec(memory_space=pltpu.VMEM)
        scalar = pl.BlockSpec(memory_space=pltpu.SMEM)

        def keep(x, shape):
            return pltpu.with_memory_space_constraint(x.reshape(shape), pltpu.HBM)

        dma = pltpu.SemaphoreType.DMA
        chips = n_row // 2
        got = pl.pallas_call(
            functools.partial(kernel, n_row, n_col, n_layer),
            out_shape=jax.ShapeDtypeStruct((BS, RB, LANES), F32),
            in_specs=[any_space] * 6 + [scalar] * 2,
            out_specs=vmem,
            scratch_shapes=(
                [pltpu.VMEM((1, slots), jnp.int32)] * 4
            ) + [
                pltpu.VMEM((n_col, slots, wide), BF16),
                pltpu.VMEM((n_row, slots, wide), BF16),
                pltpu.VMEM((n_col, 8, LANES), jnp.int32),
                pltpu.VMEM((n_row, 8, LANES), jnp.int32),
                pltpu.VMEM((8, LANES), jnp.int32),
                pltpu.VMEM((8, LANES), jnp.int32),
                pltpu.VMEM((n_row, RB * BS, 8 * BS), BF16),
                pltpu.VMEM((2, RB * BS, 8 * BS), BF16),
                pltpu.VMEM((n_row, 8 * BS, JB * BS), BF16),
                pltpu.VMEM((8 * BS, 8 * BS), BF16),
                pltpu.VMEM((RB * BS, JB * BS), F32),
                pltpu.VMEM((n_layer, RB * BS, LANES), jnp.int16),
                pltpu.VMEM((n_layer, RB * BS, LANES), jnp.int16),
                pltpu.VMEM((n_layer, 8, LANES), F32),
                pltpu.VMEM((n_layer, 8, LANES), F32),
                dma((8,)),
                dma((n_col, 2)), dma((n_col, 2)), dma((n_col,)), dma((n_col,)),
                dma((chips, 2)), dma((chips, 2)), dma((chips, 2)), dma((chips, 2)),
                dma, dma,
                dma((n_row,)), dma((n_row,)),
                dma((n_layer,)), dma((n_layer,)), dma((n_layer,)), dma((n_layer,)),
            ],
            compiler_params=pltpu.CompilerParams(
                collective_id=0, has_side_effects=True, vmem_limit_bytes=40 * 2**20
            ),
        )(
            keep(a_vals, (slots, wide)), keep(p_vals, (slots, wide)), keep(a_rows, (1, slots)), keep(a_cols, (1, slots)),
            keep(p_rows, (1, slots)), keep(p_cols, (1, slots)), a_count.reshape(1, 1), p_count.reshape(1, 1),
        )
        return got.transpose(1, 0, 2).reshape(RB * BS, LANES)

    placed = (
        P("row", "col", "layer", None, None),
        P("row", "col", "layer", None),
        P("row", "col", "layer", None),
        P("row", "col", "layer"),
    ) * 2
    return jax.shard_map(
        on_device, mesh=mesh, in_specs=placed, out_specs=P("row", ("col", "layer")), check_vma=False
    )
```

```python
import functools

import jax
import jax.numpy as jnp
from jax import lax
from jax.experimental import pallas as pl
from jax.experimental.pallas import tpu as pltpu
from jax.sharding import PartitionSpec as P

BS = 64
RB = 8
KB = 16
JB = 8
LANES = 128
HALF = BS * BS // 2
MESH = pl.DeviceIdType.MESH
F32 = jnp.float32
BF16 = jnp.bfloat16


def positions(rows, cols, count, width):
    slot = lax.broadcasted_iota(jnp.int32, rows.shape, 1)
    pos = jnp.where(slot < count, rows * width + cols, -1)
    row = jnp.concatenate([pos] * (LANES // pos.shape[1]), axis=1)
    return jnp.broadcast_to(row, (8, LANES))


def pair_onehot(pos, pairs, width, slots):
    shape = (pairs * 8, 2 * slots)
    row = lax.broadcasted_iota(jnp.int32, shape, 0)
    lane = lax.broadcasted_iota(jnp.int32, shape, 1)
    want = (row % 8) * width + 2 * (row // 8) + lane // slots
    return jnp.where(want == pos[0:1, : 2 * slots], 1.0, 0.0).astype(BF16)


def spread(vals, onehot, pairs, store, first=0, last=8):
    slots = vals.shape[0]
    low = lax.broadcasted_iota(jnp.int32, (slots, LANES), 1) < BS

    def body(step, carry):
        v = vals[:, pl.ds(pl.multiple_of(step * 512, 512), 512)].astype(F32)
        parts = []
        for g in range(4):
            a = v[:, g * LANES : (g + 1) * LANES]
            b = pltpu.roll(a, BS, 1)
            parts.append(jnp.concatenate([jnp.where(low, a, 0.0), jnp.where(low, 0.0, b)], axis=0))
            parts.append(jnp.concatenate([jnp.where(low, b, 0.0), jnp.where(low, 0.0, a)], axis=0))
        w = jnp.concatenate(parts, axis=1).astype(BF16)
        d = jnp.dot(onehot, w, preferred_element_type=F32)
        for p in range(pairs):
            rows = [d[p * 8 : (p + 1) * 8, i * LANES : (i + 1) * LANES] for i in range(8)]
            store(step, p, jnp.concatenate(rows, axis=0).astype(BF16))
        return carry

    lax.fori_loop(first, last, body, 0, unroll=True)


def quad_onehot(pos, slots):
    row = lax.broadcasted_iota(jnp.int32, (64, slots), 0)
    want = (row % 8) * JB + ((row // 8) % 2) * 4 + row // 16
    return jnp.where(want == pos[0:1, :slots], 1.0, 0.0).astype(BF16)


def lane_of(shape):
    return lax.broadcasted_iota(jnp.int32, shape, 1)


def four(lane, parts):
    low = jnp.where(lane < 32, parts[0], parts[1])
    high = jnp.where(lane < 96, parts[2], parts[3])
    return jnp.where(lane < 64, low, high)


def split(src, dst):
    slots = src.shape[0]
    first = lane_of((slots, LANES)) % BS < 32
    for t in range(16):
        a = src[:, 256 * t : 256 * t + LANES].astype(F32)
        b = src[:, 256 * t + LANES : 256 * t + 256].astype(F32)
        at = slice(t * LANES, (t + 1) * LANES)
        dst[0, :, at] = jnp.where(first, a, pltpu.roll(b, 32, 1)).astype(BF16)
        dst[1, :, at] = jnp.where(first, pltpu.roll(a, 96, 1), b).astype(BF16)


def spread_half(vals, onehot, store):
    lane = lane_of((8, LANES))
    for step in range(4):
        v = vals[:, step * 512 : (step + 1) * 512].astype(F32)
        parts = []
        for g in range(4):
            a = v[:, g * LANES : (g + 1) * LANES]
            parts += [a] + [pltpu.roll(a, 32 * r, 1) for r in range(1, 4)]
        w = jnp.concatenate(parts, axis=1).astype(BF16)
        d = jnp.dot(onehot, w, preferred_element_type=F32)
        for z in range(2):
            rows = []
            for kin in range(16):
                g, u = kin // 4, (0, 2, 1, 3)[kin % 4]
                at = [(g * 4 + (m - u) % 4) * LANES for m in range(4)]
                rows.append(
                    four(lane, [d[m * 16 + z * 8 : m * 16 + z * 8 + 8, at[m] : at[m] + LANES] for m in range(4)])
                )
            store(step, z, jnp.concatenate(rows, axis=0).astype(BF16))


def kernel(
    n_row, n_col, n_layer, a_hbm, p_hbm, *rest,
):
    small_hbm, (a_count, p_count), out, small, scratch = rest[:4], rest[4:6], rest[6], rest[7:11], rest[11:]
    (
    a_buf, p_raw, p_buf, a_pos, p_pos, a_own_pos, p_own_pos, a_dense, a_mixed, p_dense, order, acc, total,
    code, code_in, peak, peak_in,
    loc_sem, a_send, a_recv, ap_send, ap_recv, p_send, p_recv, r_send, r_recv, pp_send, pp_recv,
    c_send, c_recv, m_send, m_recv,
    ) = scratch
    row, col, lay = lax.axis_index("row"), lax.axis_index("col"), lax.axis_index("layer")
    core = lax.rem(row, 2)
    sib = row + 1 - 2 * core
    chips = n_row // 2
    slots = a_hbm.shape[0]

    barrier = pltpu.get_barrier_semaphore()
    for d in range(1, n_row):
        pl.semaphore_signal(barrier, inc=1, device_id={"row": lax.rem(row + d, n_row)}, device_id_type=MESH)
    for d in range(1, n_col):
        pl.semaphore_signal(barrier, inc=1, device_id={"col": lax.rem(col + d, n_col)}, device_id_type=MESH)
    for d in range(1, n_layer):
        pl.semaphore_signal(barrier, inc=1, device_id={"layer": lax.rem(lay + d, n_layer)}, device_id_type=MESH)
    own_a = pltpu.make_async_copy(a_hbm, a_buf.at[0], loc_sem.at[0])
    own_p = pltpu.make_async_copy(p_hbm, p_raw, loc_sem.at[1])
    tables = [pltpu.make_async_copy(small_hbm[k], small[k], loc_sem.at[2 + k]) for k in range(4)]
    own_p.start()
    for copy in tables:
        copy.start()
    own_a.start()

    def remote(src, dst, send, recv, where):
        return pltpu.make_async_remote_copy(
            src_ref=src, dst_ref=dst, send_sem=send, recv_sem=recv, device_id=where, device_id_type=MESH
        )

    def piece(ref, h):
        return ref.at[:, pl.ds(h * HALF, HALF)]

    across, shared, over, over_marks, marks = {}, {}, {}, {}, []
    for h in range(2):
        for d in range(chips):
            to = {"row": lax.rem(row + 2 * d, n_row)}
            if d:
                across[d, h] = remote(p_buf.at[0, h], p_buf.at[d, h], p_send.at[d, h], p_recv.at[d, h], to)
            mine, theirs = p_dense.at[h, 2 * d], p_dense.at[h, 2 * d + 1]
            shared[d, h] = remote(mine, theirs, r_send.at[d, h], r_recv.at[d, h], {"row": sib})
        for d in range(1, n_col):
            to = {"col": lax.rem(col + d, n_col)}
            over[d, h] = remote(piece(a_hbm, h), piece(a_buf.at[d], h), a_send.at[d, h], a_recv.at[d, h], to)
    for d in range(1, n_col):
        to = {"col": lax.rem(col + d, n_col)}
        over_marks[d] = remote(a_own_pos, a_pos.at[d], ap_send.at[d], ap_recv.at[d], to)
    for d in range(1, chips):
        to = {"row": lax.rem(row + 2 * d, n_row)}
        marks.append(remote(p_own_pos, p_pos.at[d], pp_send.at[d], pp_recv.at[d], to))

    own_p.wait()
    split(p_raw, p_buf.at[0])
    for copy in tables:
        copy.wait()
    a_rows, a_cols, p_rows, p_cols = small
    a_own_pos[...] = positions(a_rows[...], a_cols[...], a_count[0, 0], KB)
    p_own_pos[...] = positions(p_rows[...], p_cols[...], p_count[0, 0], JB)
    pl.semaphore_wait(barrier, n_row + n_col + n_layer - 3)
    for h in range(2):
        for d in range(1, chips):
            across[d, h].start()
        for d in range(1, n_col):
            over[d, h].start()
        if h == 0:
            for copy in marks + list(over_marks.values()):
                copy.start()

    shape = order.shape
    r = lax.broadcasted_iota(jnp.int32, shape, 0)
    c = lax.broadcasted_iota(jnp.int32, shape, 1)
    order[...] = jnp.where(c == (r % BS) * 8 + r // BS, 1.0, 0.0).astype(BF16)

    def take_a(d, h):
        pos = a_own_pos if d == 0 else a_pos.at[d]
        onehot = pair_onehot(pos[...], KB // 2, KB, slots)
        first = 2 * lax.rem(col - d + n_col, n_col)

        def store(step, p, rows):
            lanes = pl.ds((p % 4) * LANES, LANES)
            a_mixed[p // 4, pl.ds(pl.multiple_of(step * 64, 64), 64), lanes] = rows

        spread(a_buf.at[d], onehot, KB // 2, store, 4 * h, 4 * h + 4)
        rows = pl.ds(h * 256, 256)
        for q in range(2):
            a_dense[first + q, rows, :] = jnp.dot(
                a_mixed[q, rows, :], order[...], preferred_element_type=F32
            ).astype(BF16)

    def take_p(d, h):
        pos = p_own_pos if d == 0 else p_pos.at[d]

        def store(step, z, rows):
            p_dense[h, 2 * d, step * LANES : (step + 1) * LANES, z * LANES : (z + 1) * LANES] = rows

        spread_half(p_buf.at[d, h], quad_onehot(pos[...], slots), store)
        shared[d, h].start()

    def source(d):
        base = row if d % 2 == 0 else sib
        return lax.rem(base - 2 * (d // 2) + n_row, n_row)

    inner = jnp.logical_or(lay == 1, lay == 2)
    near = lay + 1 - 2 * lax.rem(lay, 2)
    far = lax.rem(lay + 2, 4)
    opposite = 3 - lay
    lane = lane_of((LANES, LANES))

    def multiply(first, ch, rows):
        total_ = jnp.dot(a_dense[source(0), rows, :], p_dense[ch, 0], preferred_element_type=F32)
        for d in range(1, n_row):
            total_ += jnp.dot(a_dense[source(d), rows, :], p_dense[ch, d], preferred_element_type=F32)
        for k in range(total_.shape[0] // 256):
            acc[first + k] = total_[k * 256 : (k + 1) * 256]

    def packed(k, to):
        lanes = pl.ds(pl.multiple_of((to // 2) * LANES, LANES), LANES)
        x, y = acc[k, 0:LANES, lanes], acc[k, LANES : 2 * LANES, lanes]
        odd = lax.rem(to, 2)
        stays = jnp.where(odd == 0, x, y)
        moves = pltpu.roll(jnp.where(odd == 0, y, x), BS, 1)
        return jnp.where(lane // BS == odd, stays, moves)

    def encode(k, j, x):
        top = jnp.maximum(jnp.max(jnp.abs(x), axis=0, keepdims=True), 1.2e-38)
        peak[j, k] = top
        q = jnp.round((x * (1.0 / top)) * 32767.0)
        code[j, k] = q.astype(jnp.int32).astype(jnp.int16)

    def decode(k, slot):
        q = code_in[slot, k].astype(jnp.int32).astype(F32)
        return (q * (1.0 / 32767.0)) * peak_in[slot, k]

    groups = ((0,), (1,), (2, 3))

    def hand(g, j, slot, to):
        where, ks = {"layer": to}, pl.ds(groups[g][0], len(groups[g]))
        return (
            remote(code.at[j, ks], code_in.at[slot, ks], c_send.at[g, j], c_recv.at[g, slot], where),
            remote(peak.at[j, ks], peak_in.at[slot, ks], m_send.at[g, j], m_recv.at[g, slot], where),
        )

    def via(g):
        return hand(g, 0, jnp.where(inner, 3, 0), jnp.where(inner, opposite, near))

    def start(copies):
        for copy in copies:
            copy.start()

    def arrive(copies):
        for copy in copies:
            copy.wait_recv()

    def ready(g):
        for k in groups[g]:
            encode(k, 0, packed(k, opposite))
        start(via(g))

        @pl.when(jnp.logical_not(inner))
        def _():
            for k in groups[g]:
                encode(k, 2, packed(k, far))
            start(hand(g, 2, 2, far))

        for k in groups[g]:
            encode(k, 1, packed(k, near))
            total[k] = packed(k, lay)

    def send_near(g):
        start(hand(g, 1, 1, near))

    def forward(g):
        @pl.when(inner)
        def _():
            arrive(hand(g, 0, 0, near))
            for k in groups[g]:
                encode(k, 2, packed(k, far) + decode(k, 0))
            start(hand(g, 2, 2, far))

    def collect(g):
        @pl.when(inner)
        def _():
            arrive(hand(g, 0, 3, opposite))
            for k in groups[g]:
                total[k] += decode(k, 3)

        arrive(hand(g, 1, 1, near))
        for k in groups[g]:
            total[k] += decode(k, 1)
        arrive(hand(g, 2, 2, far))
        for k in groups[g]:
            total[k] += decode(k, 2)

    def fill(h):
        for d in range(1, chips):
            if h == 0:
                marks[d - 1].wait_recv()
            across[d, h].wait_recv()
            take_p(d, h)
        for d in range(1, n_col):
            if h == 0:
                over_marks[d].wait_recv()
            over[d, h].wait_recv()
            take_a(d, h)

    own_a.wait()
    take_p(0, 0)
    take_a(0, 0)
    take_p(0, 1)
    take_a(0, 1)
    fill(0)
    for d in range(chips):
        shared[d, 0].wait_recv()
    multiply(0, 0, pl.ds(0, 256))
    ready(0)
    send_near(0)
    fill(1)
    multiply(1, 0, pl.ds(256, 256))
    ready(1)
    forward(0)
    for d in range(chips):
        shared[d, 1].wait_recv()
    multiply(2, 1, pl.ds(0, 512))
    ready(2)
    send_near(1)
    forward(1)
    send_near(2)
    forward(2)
    for g in range(3):
        collect(g)
    for rh in range(2):
        f, g = total[rh], total[2 + rh]
        for s in range(2):
            if s == 0:
                x = four(lane, [f, pltpu.roll(g, 32, 1), pltpu.roll(f, 32, 1), pltpu.roll(g, 64, 1)])
            else:
                x = four(lane, [pltpu.roll(f, 64, 1), pltpu.roll(g, 96, 1), pltpu.roll(f, 96, 1), g])
            out[pl.ds(rh * 32 + s * 16, 16)] = x.reshape(16, 8, LANES)

    sums = []
    for g in range(3):
        sums += list(via(g)) + list(hand(g, 2, 2, far)) + list(hand(g, 1, 1, near))
    for copy in list(across.values()) + list(shared.values()) + list(over.values()) + list(over_marks.values()):
        copy.wait_send()
    for copy in marks + sums:
        copy.wait_send()


def solution(mesh):
    n_row, n_col, n_layer = (mesh.shape[k] for k in ("row", "col", "layer"))

    def on_device(a_vals, a_rows, a_cols, a_count, p_vals, p_rows, p_cols, p_count):
        slots = a_vals.shape[3]
        wide = BS * BS
        any_space = pl.BlockSpec(memory_space=pltpu.HBM)
        vmem = pl.BlockSpec(memory_space=pltpu.VMEM)
        scalar = pl.BlockSpec(memory_space=pltpu.SMEM)

        def keep(x, shape):
            return pltpu.with_memory_space_constraint(x.reshape(shape), pltpu.HBM)

        dma = pltpu.SemaphoreType.DMA
        chips = n_row // 2
        got = pl.pallas_call(
            functools.partial(kernel, n_row, n_col, n_layer),
            out_shape=jax.ShapeDtypeStruct((BS, RB, LANES), F32),
            in_specs=[any_space] * 6 + [scalar] * 2,
            out_specs=vmem,
            scratch_shapes=(
                [pltpu.VMEM((1, slots), jnp.int32)] * 4
            ) + [
                pltpu.VMEM((n_col, slots, wide), BF16),
                pltpu.VMEM((slots, wide), BF16),
                pltpu.VMEM((chips, 2, slots, HALF), BF16),
                pltpu.VMEM((n_col, 8, LANES), jnp.int32),
                pltpu.VMEM((chips, 8, LANES), jnp.int32),
                pltpu.VMEM((8, LANES), jnp.int32),
                pltpu.VMEM((8, LANES), jnp.int32),
                pltpu.VMEM((n_row, RB * BS, 8 * BS), BF16),
                pltpu.VMEM((2, RB * BS, 8 * BS), BF16),
                pltpu.VMEM((2, n_row, 8 * BS, JB * BS // 2), BF16),
                pltpu.VMEM((8 * BS, 8 * BS), BF16),
                pltpu.VMEM((4, 256, 256), F32),
                pltpu.VMEM((4, LANES, LANES), F32),
                pltpu.VMEM((3, 4, LANES, LANES), jnp.int16),
                pltpu.VMEM((4, 4, LANES, LANES), jnp.int16),
                pltpu.VMEM((3, 4, 1, LANES), F32),
                pltpu.VMEM((4, 4, 1, LANES), F32),
                dma((8,)),
                dma((n_col, 2)), dma((n_col, 2)), dma((n_col,)), dma((n_col,)),
                dma((chips, 2)), dma((chips, 2)), dma((chips, 2)), dma((chips, 2)),
                dma((chips,)), dma((chips,)),
                dma((3, 3)), dma((3, 4)), dma((3, 3)), dma((3, 4)),
            ],
            compiler_params=pltpu.CompilerParams(
                collective_id=0, has_side_effects=True, vmem_limit_bytes=40 * 2**20
            ),
        )(
            keep(a_vals, (slots, wide)), keep(p_vals, (slots, wide)), keep(a_rows, (1, slots)), keep(a_cols, (1, slots)),
            keep(p_rows, (1, slots)), keep(p_cols, (1, slots)), a_count.reshape(1, 1), p_count.reshape(1, 1),
        )
        return got.transpose(1, 0, 2).reshape(RB * BS, LANES)

    placed = (
        P("row", "col", "layer", None, None),
        P("row", "col", "layer", None),
        P("row", "col", "layer", None),
        P("row", "col", "layer"),
    ) * 2
    return jax.shard_map(
        on_device, mesh=mesh, in_specs=placed, out_specs=P("row", ("col", "layer")), check_vma=False
    )
```

```python
import functools

import jax
import jax.numpy as jnp
from jax import lax
from jax.experimental import pallas as pl
from jax.experimental.pallas import tpu as pltpu
from jax.sharding import PartitionSpec as P

BS = 64
RB = 8
KB = 16
JB = 8
LANES = 128
HALF = BS * BS // 2
MESH = pl.DeviceIdType.MESH
F32 = jnp.float32
BF16 = jnp.bfloat16


def positions(rows, cols, count, width):
    slot = lax.broadcasted_iota(jnp.int32, rows.shape, 1)
    pos = jnp.where(slot < count, rows * width + cols, -1)
    row = jnp.concatenate([pos] * (LANES // pos.shape[1]), axis=1)
    return jnp.broadcast_to(row, (8, LANES))


def pair_onehot(pos, pairs, width, slots):
    shape = (pairs * 8, 2 * slots)
    row = lax.broadcasted_iota(jnp.int32, shape, 0)
    lane = lax.broadcasted_iota(jnp.int32, shape, 1)
    want = (row % 8) * width + 2 * (row // 8) + lane // slots
    return jnp.where(want == pos[0:1, : 2 * slots], 1.0, 0.0).astype(BF16)


def spread(vals, onehot, pairs, store, first=0, last=8):
    slots = vals.shape[0]
    low = lax.broadcasted_iota(jnp.int32, (slots, LANES), 1) < BS

    def body(step, carry):
        v = vals[:, pl.ds(pl.multiple_of(step * 512, 512), 512)].astype(F32)
        parts = []
        for g in range(4):
            a = v[:, g * LANES : (g + 1) * LANES]
            b = pltpu.roll(a, BS, 1)
            parts.append(jnp.concatenate([jnp.where(low, a, 0.0), jnp.where(low, 0.0, b)], axis=0))
            parts.append(jnp.concatenate([jnp.where(low, b, 0.0), jnp.where(low, 0.0, a)], axis=0))
        w = jnp.concatenate(parts, axis=1).astype(BF16)
        d = jnp.dot(onehot, w, preferred_element_type=F32)
        for p in range(pairs):
            rows = [d[p * 8 : (p + 1) * 8, i * LANES : (i + 1) * LANES] for i in range(8)]
            store(step, p, jnp.concatenate(rows, axis=0).astype(BF16))
        return carry

    lax.fori_loop(first, last, body, 0, unroll=True)


def quad_onehot(pos, slots):
    row = lax.broadcasted_iota(jnp.int32, (64, slots), 0)
    want = (row % 8) * JB + ((row // 8) % 2) * 4 + row // 16
    return jnp.where(want == pos[0:1, :slots], 1.0, 0.0).astype(BF16)


def lane_of(shape):
    return lax.broadcasted_iota(jnp.int32, shape, 1)


def four(lane, parts):
    low = jnp.where(lane < 32, parts[0], parts[1])
    high = jnp.where(lane < 96, parts[2], parts[3])
    return jnp.where(lane < 64, low, high)


def split(src, dst):
    slots = src.shape[0]
    first = lane_of((slots, LANES)) % BS < 32
    for t in range(16):
        a = src[:, 256 * t : 256 * t + LANES].astype(F32)
        b = src[:, 256 * t + LANES : 256 * t + 256].astype(F32)
        at = slice(t * LANES, (t + 1) * LANES)
        dst[0, :, at] = jnp.where(first, a, pltpu.roll(b, 32, 1)).astype(BF16)
        dst[1, :, at] = jnp.where(first, pltpu.roll(a, 96, 1), b).astype(BF16)


def spread_half(vals, onehot, store):
    lane = lane_of((8, LANES))
    for step in range(4):
        v = vals[:, step * 512 : (step + 1) * 512].astype(F32)
        parts = []
        for g in range(4):
            a = v[:, g * LANES : (g + 1) * LANES]
            parts += [a] + [pltpu.roll(a, 32 * r, 1) for r in range(1, 4)]
        w = jnp.concatenate(parts, axis=1).astype(BF16)
        d = jnp.dot(onehot, w, preferred_element_type=F32)
        for z in range(2):
            rows = []
            for kin in range(16):
                g, u = kin // 4, (0, 2, 1, 3)[kin % 4]
                at = [(g * 4 + (m - u) % 4) * LANES for m in range(4)]
                rows.append(
                    four(lane, [d[m * 16 + z * 8 : m * 16 + z * 8 + 8, at[m] : at[m] + LANES] for m in range(4)])
                )
            store(step, z, jnp.concatenate(rows, axis=0).astype(BF16))


def kernel(
    n_row, n_col, n_layer, a_hbm, p_hbm, *rest,
):
    small_hbm, (a_count, p_count), out, small, scratch = rest[:4], rest[4:6], rest[6], rest[7:11], rest[11:]
    (
    a_buf, p_raw, p_buf, a_pos, p_pos, a_own_pos, p_own_pos, a_dense, a_mixed, p_dense, order, acc, total,
    code, code_in, peak, peak_in,
    loc_sem, a_send, a_recv, ap_send, ap_recv, p_send, p_recv, r_send, r_recv, pp_send, pp_recv,
    c_send, c_recv, m_send, m_recv,
    ) = scratch
    row, col, lay = lax.axis_index("row"), lax.axis_index("col"), lax.axis_index("layer")
    core = lax.rem(row, 2)
    sib = row + 1 - 2 * core
    chips = n_row // 2
    slots = a_hbm.shape[0]

    barrier = pltpu.get_barrier_semaphore()
    for d in range(1, n_row):
        pl.semaphore_signal(barrier, inc=1, device_id={"row": lax.rem(row + d, n_row)}, device_id_type=MESH)
    for d in range(1, n_col):
        pl.semaphore_signal(barrier, inc=1, device_id={"col": lax.rem(col + d, n_col)}, device_id_type=MESH)
    for d in range(1, n_layer):
        pl.semaphore_signal(barrier, inc=1, device_id={"layer": lax.rem(lay + d, n_layer)}, device_id_type=MESH)
    own_a = pltpu.make_async_copy(a_hbm, a_buf.at[0], loc_sem.at[0])
    own_p = pltpu.make_async_copy(p_hbm, p_raw, loc_sem.at[1])
    tables = [pltpu.make_async_copy(small_hbm[k], small[k], loc_sem.at[2 + k]) for k in range(4)]
    own_p.start()
    for copy in tables:
        copy.start()
    own_a.start()

    def remote(src, dst, send, recv, where):
        return pltpu.make_async_remote_copy(
            src_ref=src, dst_ref=dst, send_sem=send, recv_sem=recv, device_id=where, device_id_type=MESH
        )

    def piece(ref, h):
        return ref.at[:, pl.ds(h * HALF, HALF)]

    across, shared, over, over_marks, marks = {}, {}, {}, {}, []
    for h in range(2):
        for d in range(chips):
            to = {"row": lax.rem(row + 2 * d, n_row)}
            if d:
                across[d, h] = remote(p_buf.at[0, h], p_buf.at[d, h], p_send.at[d, h], p_recv.at[d, h], to)
            mine, theirs = p_dense.at[h, 2 * d], p_dense.at[h, 2 * d + 1]
            shared[d, h] = remote(mine, theirs, r_send.at[d, h], r_recv.at[d, h], {"row": sib})
        for d in range(1, n_col):
            to = {"col": lax.rem(col + d, n_col)}
            over[d, h] = remote(piece(a_hbm, h), piece(a_buf.at[d], h), a_send.at[d, h], a_recv.at[d, h], to)
    for d in range(1, n_col):
        to = {"col": lax.rem(col + d, n_col)}
        over_marks[d] = remote(a_own_pos, a_pos.at[d], ap_send.at[d], ap_recv.at[d], to)
    for d in range(1, chips):
        to = {"row": lax.rem(row + 2 * d, n_row)}
        marks.append(remote(p_own_pos, p_pos.at[d], pp_send.at[d], pp_recv.at[d], to))

    own_p.wait()
    split(p_raw, p_buf.at[0])
    for copy in tables:
        copy.wait()
    a_rows, a_cols, p_rows, p_cols = small
    a_own_pos[...] = positions(a_rows[...], a_cols[...], a_count[0, 0], KB)
    p_own_pos[...] = positions(p_rows[...], p_cols[...], p_count[0, 0], JB)
    pl.semaphore_wait(barrier, n_row + n_col + n_layer - 3)
    for h in range(2):
        for d in range(1, chips):
            across[d, h].start()
        for d in range(1, n_col):
            over[d, h].start()
        if h == 0:
            for copy in marks + list(over_marks.values()):
                copy.start()

    shape = order.shape
    r = lax.broadcasted_iota(jnp.int32, shape, 0)
    c = lax.broadcasted_iota(jnp.int32, shape, 1)
    order[...] = jnp.where(c == (r % BS) * 8 + r // BS, 1.0, 0.0).astype(BF16)

    def take_a(d, h):
        pos = a_own_pos if d == 0 else a_pos.at[d]
        onehot = pair_onehot(pos[...], KB // 2, KB, slots)
        first = 2 * lax.rem(col - d + n_col, n_col)

        def store(step, p, rows):
            lanes = pl.ds((p % 4) * LANES, LANES)
            a_mixed[p // 4, pl.ds(pl.multiple_of(step * 64, 64), 64), lanes] = rows

        spread(a_buf.at[d], onehot, KB // 2, store, 4 * h, 4 * h + 4)
        rows = pl.ds(h * 256, 256)
        for q in range(2):
            a_dense[first + q, rows, :] = jnp.dot(
                a_mixed[q, rows, :], order[...], preferred_element_type=F32
            ).astype(BF16)

    def take_p(d, h):
        pos = p_own_pos if d == 0 else p_pos.at[d]

        def store(step, z, rows):
            p_dense[h, 2 * d, step * LANES : (step + 1) * LANES, z * LANES : (z + 1) * LANES] = rows

        spread_half(p_buf.at[d, h], quad_onehot(pos[...], slots), store)
        shared[d, h].start()

    def source(d):
        base = row if d % 2 == 0 else sib
        return lax.rem(base - 2 * (d // 2) + n_row, n_row)

    inner = jnp.logical_or(lay == 1, lay == 2)
    near = lay + 1 - 2 * lax.rem(lay, 2)
    far = lax.rem(lay + 2, 4)
    opposite = 3 - lay
    lane = lane_of((LANES, LANES))

    def multiply(first, ch, rows):
        total_ = jnp.dot(a_dense[source(0), rows, :], p_dense[ch, 0], preferred_element_type=F32)
        for d in range(1, n_row):
            total_ += jnp.dot(a_dense[source(d), rows, :], p_dense[ch, d], preferred_element_type=F32)
        for k in range(total_.shape[0] // 256):
            acc[first + k] = total_[k * 256 : (k + 1) * 256]

    def packed(k, to):
        lanes = pl.ds(pl.multiple_of((to // 2) * LANES, LANES), LANES)
        x, y = acc[k, 0:LANES, lanes], acc[k, LANES : 2 * LANES, lanes]
        odd = lax.rem(to, 2)
        stays = jnp.where(odd == 0, x, y)
        moves = pltpu.roll(jnp.where(odd == 0, y, x), BS, 1)
        return jnp.where(lane // BS == odd, stays, moves)

    def encode(k, j, x):
        top = jnp.maximum(jnp.max(jnp.abs(x), axis=0, keepdims=True), 1.2e-38)
        peak[j, k] = top
        q = jnp.round((x * (1.0 / top)) * 32767.0)
        code[j, k] = q.astype(jnp.int32).astype(jnp.int16)

    def decode(k, slot):
        q = code_in[slot, k].astype(jnp.int32).astype(F32)
        return (q * (1.0 / 32767.0)) * peak_in[slot, k]

    groups = ((0,), (1,), (2, 3))

    def hand(g, j, slot, to):
        where, ks = {"layer": to}, pl.ds(groups[g][0], len(groups[g]))
        return (
            remote(code.at[j, ks], code_in.at[slot, ks], c_send.at[g, j], c_recv.at[g, slot], where),
            remote(peak.at[j, ks], peak_in.at[slot, ks], m_send.at[g, j], m_recv.at[g, slot], where),
        )

    def via(g):
        return hand(g, 0, jnp.where(inner, 3, 0), jnp.where(inner, opposite, near))

    def start(copies):
        for copy in copies:
            copy.start()

    def arrive(copies):
        for copy in copies:
            copy.wait_recv()

    both = (0, 1, 2)

    def give(g, j, slot, to):
        for k in groups[g]:
            encode(k, j, packed(k, to))
        return hand(g, j, slot, near if slot == 4 else to)

    def give_far(g):
        start(give(g, 2, 4 if g in both else 2, far))

    def give_via(g):
        for k in groups[g]:
            encode(k, 0, packed(k, opposite))
        start(via(g))

    def ready(g):
        if g in both:
            pl.when(jnp.logical_not(inner))(functools.partial(give_via, g))
        else:
            give_via(g)
        pl.when(jnp.logical_not(inner))(functools.partial(give_far, g))
        for k in groups[g]:
            total[k] = packed(k, lay)

    def send_near(g):
        start(give(g, 1, 1, near))

    def forward(g):
        @pl.when(inner)
        def _():
            arrive(hand(g, 0, 0, near))
            for k in groups[g]:
                encode(k, 2, packed(k, far) + decode(k, 0))
            start(hand(g, 2, 2, far))
            if g in both:
                arrive(hand(g, 0, 4, near))
                for k in groups[g]:
                    encode(k, 0, packed(k, opposite) + decode(k, 4))
                start(hand(g, 0, 3, opposite))

    def add(g, slot, to):
        arrive(hand(g, 0, slot, to))
        for k in groups[g]:
            total[k] += decode(k, slot)

    def collect(g):
        pl.when(inner)(functools.partial(add, g, 3, opposite))
        add(g, 1, near)
        if g in both:
            pl.when(jnp.logical_not(inner))(functools.partial(add, g, 2, far))
        else:
            add(g, 2, far)

    def fill(h):
        for d in range(1, chips):
            if h == 0:
                marks[d - 1].wait_recv()
            across[d, h].wait_recv()
            take_p(d, h)
        for d in range(1, n_col):
            if h == 0:
                over_marks[d].wait_recv()
            over[d, h].wait_recv()
            take_a(d, h)

    own_a.wait()
    take_p(0, 0)
    take_a(0, 0)
    take_p(0, 1)
    take_a(0, 1)
    fill(0)
    for d in range(chips):
        shared[d, 0].wait_recv()
    multiply(0, 0, pl.ds(0, 256))
    ready(0)
    send_near(0)
    fill(1)
    multiply(1, 0, pl.ds(256, 256))
    ready(1)
    forward(0)
    for d in range(chips):
        shared[d, 1].wait_recv()
    multiply(2, 1, pl.ds(0, 512))
    ready(2)
    send_near(1)
    send_near(2)
    forward(1)
    forward(2)
    for g in range(3):
        collect(g)
    for rh in range(2):
        f, g = total[rh], total[2 + rh]
        for s in range(2):
            if s == 0:
                x = four(lane, [f, pltpu.roll(g, 32, 1), pltpu.roll(f, 32, 1), pltpu.roll(g, 64, 1)])
            else:
                x = four(lane, [pltpu.roll(f, 64, 1), pltpu.roll(g, 96, 1), pltpu.roll(f, 96, 1), g])
            out[pl.ds(rh * 32 + s * 16, 16)] = x.reshape(16, 8, LANES)

    sums = []
    for g in range(3):
        sums += list(via(g)) + list(hand(g, 2, 2, far)) + list(hand(g, 1, 1, near))
    for copy in list(across.values()) + list(shared.values()) + list(over.values()) + list(over_marks.values()):
        copy.wait_send()
    for copy in marks + sums:
        copy.wait_send()


def solution(mesh):
    n_row, n_col, n_layer = (mesh.shape[k] for k in ("row", "col", "layer"))

    def on_device(a_vals, a_rows, a_cols, a_count, p_vals, p_rows, p_cols, p_count):
        slots = a_vals.shape[3]
        wide = BS * BS
        any_space = pl.BlockSpec(memory_space=pltpu.HBM)
        vmem = pl.BlockSpec(memory_space=pltpu.VMEM)
        scalar = pl.BlockSpec(memory_space=pltpu.SMEM)

        def keep(x, shape):
            return pltpu.with_memory_space_constraint(x.reshape(shape), pltpu.HBM)

        dma = pltpu.SemaphoreType.DMA
        chips = n_row // 2
        got = pl.pallas_call(
            functools.partial(kernel, n_row, n_col, n_layer),
            out_shape=jax.ShapeDtypeStruct((BS, RB, LANES), F32),
            in_specs=[any_space] * 6 + [scalar] * 2,
            out_specs=vmem,
            scratch_shapes=(
                [pltpu.VMEM((1, slots), jnp.int32)] * 4
            ) + [
                pltpu.VMEM((n_col, slots, wide), BF16),
                pltpu.VMEM((slots, wide), BF16),
                pltpu.VMEM((chips, 2, slots, HALF), BF16),
                pltpu.VMEM((n_col, 8, LANES), jnp.int32),
                pltpu.VMEM((chips, 8, LANES), jnp.int32),
                pltpu.VMEM((8, LANES), jnp.int32),
                pltpu.VMEM((8, LANES), jnp.int32),
                pltpu.VMEM((n_row, RB * BS, 8 * BS), BF16),
                pltpu.VMEM((2, RB * BS, 8 * BS), BF16),
                pltpu.VMEM((2, n_row, 8 * BS, JB * BS // 2), BF16),
                pltpu.VMEM((8 * BS, 8 * BS), BF16),
                pltpu.VMEM((4, 256, 256), F32),
                pltpu.VMEM((4, LANES, LANES), F32),
                pltpu.VMEM((3, 4, LANES, LANES), jnp.int16),
                pltpu.VMEM((5, 4, LANES, LANES), jnp.int16),
                pltpu.VMEM((3, 4, 1, LANES), F32),
                pltpu.VMEM((5, 4, 1, LANES), F32),
                dma((8,)),
                dma((n_col, 2)), dma((n_col, 2)), dma((n_col,)), dma((n_col,)),
                dma((chips, 2)), dma((chips, 2)), dma((chips, 2)), dma((chips, 2)),
                dma((chips,)), dma((chips,)),
                dma((3, 3)), dma((3, 5)), dma((3, 3)), dma((3, 5)),
            ],
            compiler_params=pltpu.CompilerParams(
                collective_id=0, has_side_effects=True, vmem_limit_bytes=40 * 2**20
            ),
        )(
            keep(a_vals, (slots, wide)), keep(p_vals, (slots, wide)), keep(a_rows, (1, slots)), keep(a_cols, (1, slots)),
            keep(p_rows, (1, slots)), keep(p_cols, (1, slots)), a_count.reshape(1, 1), p_count.reshape(1, 1),
        )
        return got.transpose(1, 0, 2).reshape(RB * BS, LANES)

    placed = (
        P("row", "col", "layer", None, None),
        P("row", "col", "layer", None),
        P("row", "col", "layer", None),
        P("row", "col", "layer"),
    ) * 2
    return jax.shard_map(
        on_device, mesh=mesh, in_specs=placed, out_specs=P("row", ("col", "layer")), check_vma=False
    )
```

```python
import functools

import jax
import jax.numpy as jnp
from jax import lax
from jax.experimental import pallas as pl
from jax.experimental.pallas import tpu as pltpu
from jax.sharding import PartitionSpec as P

BS = 64
RB = 8
KB = 16
JB = 8
LANES = 128
HALF = BS * BS // 2
MESH = pl.DeviceIdType.MESH
F32 = jnp.float32
BF16 = jnp.bfloat16


def positions(rows, cols, count, width):
    slot = lax.broadcasted_iota(jnp.int32, rows.shape, 1)
    pos = jnp.where(slot < count, rows * width + cols, -1)
    row = jnp.concatenate([pos] * (LANES // pos.shape[1]), axis=1)
    return jnp.broadcast_to(row, (8, LANES))


def pair_onehot(pos, pairs, width, slots):
    shape = (pairs * 8, 2 * slots)
    row = lax.broadcasted_iota(jnp.int32, shape, 0)
    lane = lax.broadcasted_iota(jnp.int32, shape, 1)
    want = (row % 8) * width + 2 * (row // 8) + lane // slots
    return jnp.where(want == pos[0:1, : 2 * slots], 1.0, 0.0).astype(BF16)


def spread(vals, onehot, pairs, store, first=0, last=8):
    slots = vals.shape[0]
    low = lax.broadcasted_iota(jnp.int32, (slots, LANES), 1) < BS

    def body(step, carry):
        v = vals[:, pl.ds(pl.multiple_of(step * 512, 512), 512)].astype(F32)
        parts = []
        for g in range(4):
            a = v[:, g * LANES : (g + 1) * LANES]
            b = pltpu.roll(a, BS, 1)
            parts.append(jnp.concatenate([jnp.where(low, a, 0.0), jnp.where(low, 0.0, b)], axis=0))
            parts.append(jnp.concatenate([jnp.where(low, b, 0.0), jnp.where(low, 0.0, a)], axis=0))
        w = jnp.concatenate(parts, axis=1).astype(BF16)
        d = jnp.dot(onehot, w, preferred_element_type=F32)
        for p in range(pairs):
            rows = [d[p * 8 : (p + 1) * 8, i * LANES : (i + 1) * LANES] for i in range(8)]
            store(step, p, jnp.concatenate(rows, axis=0).astype(BF16))
        return carry

    lax.fori_loop(first, last, body, 0, unroll=True)


def quad_onehot(pos, slots):
    row = lax.broadcasted_iota(jnp.int32, (64, slots), 0)
    want = (row % 8) * JB + ((row // 8) % 2) * 4 + row // 16
    return jnp.where(want == pos[0:1, :slots], 1.0, 0.0).astype(BF16)


def lane_of(shape):
    return lax.broadcasted_iota(jnp.int32, shape, 1)


def four(lane, parts):
    low = jnp.where(lane < 32, parts[0], parts[1])
    high = jnp.where(lane < 96, parts[2], parts[3])
    return jnp.where(lane < 64, low, high)


def split(src, dst):
    slots = src.shape[0]
    first = lane_of((slots, LANES)) % BS < 32
    for t in range(16):
        a = src[:, 256 * t : 256 * t + LANES].astype(F32)
        b = src[:, 256 * t + LANES : 256 * t + 256].astype(F32)
        at = slice(t * LANES, (t + 1) * LANES)
        dst[0, :, at] = jnp.where(first, a, pltpu.roll(b, 32, 1)).astype(BF16)
        dst[1, :, at] = jnp.where(first, pltpu.roll(a, 96, 1), b).astype(BF16)


def spread_half(vals, onehot, store):
    lane = lane_of((8, LANES))
    for step in range(4):
        v = vals[:, step * 512 : (step + 1) * 512].astype(F32)
        parts = []
        for g in range(4):
            a = v[:, g * LANES : (g + 1) * LANES]
            parts += [a] + [pltpu.roll(a, 32 * r, 1) for r in range(1, 4)]
        w = jnp.concatenate(parts, axis=1).astype(BF16)
        d = jnp.dot(onehot, w, preferred_element_type=F32)
        for z in range(2):
            rows = []
            for kin in range(16):
                g, u = kin // 4, (0, 2, 1, 3)[kin % 4]
                at = [(g * 4 + (m - u) % 4) * LANES for m in range(4)]
                rows.append(
                    four(lane, [d[m * 16 + z * 8 : m * 16 + z * 8 + 8, at[m] : at[m] + LANES] for m in range(4)])
                )
            store(step, z, jnp.concatenate(rows, axis=0).astype(BF16))


def kernel(
    n_row, n_col, n_layer, a_hbm, p_hbm, *rest,
):
    small_hbm, (a_count, p_count), out, small, scratch = rest[:4], rest[4:6], rest[6], rest[7:11], rest[11:]
    (
    a_buf, p_raw, p_buf, a_pos, p_pos, a_own_pos, p_own_pos, a_dense, a_mixed, p_dense, order, acc, total,
    code, code_in, peak, peak_in,
    loc_sem, a_send, a_recv, ap_send, ap_recv, p_send, p_recv, r_send, r_recv, pp_send, pp_recv,
    c_send, c_recv, m_send, m_recv,
    ) = scratch
    row, col, lay = lax.axis_index("row"), lax.axis_index("col"), lax.axis_index("layer")
    core = lax.rem(row, 2)
    sib = row + 1 - 2 * core
    chips = n_row // 2
    slots = a_hbm.shape[0]

    barrier = pltpu.get_barrier_semaphore()
    for d in range(1, n_row):
        pl.semaphore_signal(barrier, inc=1, device_id={"row": lax.rem(row + d, n_row)}, device_id_type=MESH)
    for d in range(1, n_col):
        pl.semaphore_signal(barrier, inc=1, device_id={"col": lax.rem(col + d, n_col)}, device_id_type=MESH)
    for d in range(1, n_layer):
        pl.semaphore_signal(barrier, inc=1, device_id={"layer": lax.rem(lay + d, n_layer)}, device_id_type=MESH)
    own_a = pltpu.make_async_copy(a_hbm, a_buf.at[0], loc_sem.at[0])
    own_p = pltpu.make_async_copy(p_hbm, p_raw, loc_sem.at[1])
    tables = [pltpu.make_async_copy(small_hbm[k], small[k], loc_sem.at[2 + k]) for k in range(4)]
    own_p.start()
    for copy in tables:
        copy.start()
    own_a.start()

    def remote(src, dst, send, recv, where):
        return pltpu.make_async_remote_copy(
            src_ref=src, dst_ref=dst, send_sem=send, recv_sem=recv, device_id=where, device_id_type=MESH
        )

    def piece(ref, h):
        return ref.at[:, pl.ds(h * HALF, HALF)]

    across, shared, over, over_marks, marks = {}, {}, {}, {}, []
    for h in range(2):
        for d in range(chips):
            to = {"row": lax.rem(row + 2 * d, n_row)}
            if d:
                across[d, h] = remote(p_buf.at[0, h], p_buf.at[d, h], p_send.at[d, h], p_recv.at[d, h], to)
            mine, theirs = p_dense.at[h, 2 * d], p_dense.at[h, 2 * d + 1]
            shared[d, h] = remote(mine, theirs, r_send.at[d, h], r_recv.at[d, h], {"row": sib})
        for d in range(1, n_col):
            to = {"col": lax.rem(col + d, n_col)}
            over[d, h] = remote(piece(a_hbm, h), piece(a_buf.at[d], h), a_send.at[d, h], a_recv.at[d, h], to)
    for d in range(1, n_col):
        to = {"col": lax.rem(col + d, n_col)}
        over_marks[d] = remote(a_own_pos, a_pos.at[d], ap_send.at[d], ap_recv.at[d], to)
    for d in range(1, chips):
        to = {"row": lax.rem(row + 2 * d, n_row)}
        marks.append(remote(p_own_pos, p_pos.at[d], pp_send.at[d], pp_recv.at[d], to))

    own_p.wait()
    split(p_raw, p_buf.at[0])
    for copy in tables:
        copy.wait()
    a_rows, a_cols, p_rows, p_cols = small
    a_own_pos[...] = positions(a_rows[...], a_cols[...], a_count[0, 0], KB)
    p_own_pos[...] = positions(p_rows[...], p_cols[...], p_count[0, 0], JB)
    pl.semaphore_wait(barrier, n_row + n_col + n_layer - 3)
    for h in range(2):
        for d in range(1, chips):
            across[d, h].start()
        for d in range(1, n_col):
            over[d, h].start()
        if h == 0:
            for copy in marks + list(over_marks.values()):
                copy.start()

    shape = order.shape
    r = lax.broadcasted_iota(jnp.int32, shape, 0)
    c = lax.broadcasted_iota(jnp.int32, shape, 1)
    order[...] = jnp.where(c == (r % BS) * 8 + r // BS, 1.0, 0.0).astype(BF16)

    def take_a(d, h):
        pos = a_own_pos if d == 0 else a_pos.at[d]
        onehot = pair_onehot(pos[...], KB // 2, KB, slots)
        first = 2 * lax.rem(col - d + n_col, n_col)

        def store(step, p, rows):
            lanes = pl.ds((p % 4) * LANES, LANES)
            a_mixed[p // 4, pl.ds(pl.multiple_of(step * 64, 64), 64), lanes] = rows

        spread(a_buf.at[d], onehot, KB // 2, store, 4 * h, 4 * h + 4)
        rows = pl.ds(h * 256, 256)
        for q in range(2):
            a_dense[first + q, rows, :] = jnp.dot(
                a_mixed[q, rows, :], order[...], preferred_element_type=F32
            ).astype(BF16)

    def take_p(d, h):
        pos = p_own_pos if d == 0 else p_pos.at[d]

        def store(step, z, rows):
            p_dense[h, 2 * d, step * LANES : (step + 1) * LANES, z * LANES : (z + 1) * LANES] = rows

        spread_half(p_buf.at[d, h], quad_onehot(pos[...], slots), store)
        shared[d, h].start()

    def source(d):
        base = row if d % 2 == 0 else sib
        return lax.rem(base - 2 * (d // 2) + n_row, n_row)

    inner = jnp.logical_or(lay == 1, lay == 2)
    near = lay + 1 - 2 * lax.rem(lay, 2)
    far = lax.rem(lay + 2, 4)
    opposite = 3 - lay
    lane = lane_of((LANES, LANES))

    def multiply(first, ch, rows):
        total_ = jnp.dot(a_dense[source(0), rows, :], p_dense[ch, 0], preferred_element_type=F32)
        for d in range(1, n_row):
            total_ += jnp.dot(a_dense[source(d), rows, :], p_dense[ch, d], preferred_element_type=F32)
        for k in range(total_.shape[0] // 256):
            acc[first + k] = total_[k * 256 : (k + 1) * 256]

    def packed(k, to):
        lanes = pl.ds(pl.multiple_of((to // 2) * LANES, LANES), LANES)
        x, y = acc[k, 0:LANES, lanes], acc[k, LANES : 2 * LANES, lanes]
        odd = lax.rem(to, 2)
        stays = jnp.where(odd == 0, x, y)
        moves = pltpu.roll(jnp.where(odd == 0, y, x), BS, 1)
        return jnp.where(lane // BS == odd, stays, moves)

    def encode(k, j, x):
        top = jnp.maximum(jnp.max(jnp.abs(x), axis=0, keepdims=True), 1.2e-38)
        peak[j, k] = top
        q = jnp.round((x * (1.0 / top)) * 32767.0)
        code[j, k] = q.astype(jnp.int32).astype(jnp.int16)

    def decode(k, slot):
        q = code_in[slot, k].astype(jnp.int32).astype(F32)
        return (q * (1.0 / 32767.0)) * peak_in[slot, k]

    groups = ((0,), (1,), (2, 3))

    def hand(g, j, slot, to):
        where, ks = {"layer": to}, pl.ds(groups[g][0], len(groups[g]))
        return (
            remote(code.at[j, ks], code_in.at[slot, ks], c_send.at[g, j], c_recv.at[g, slot], where),
            remote(peak.at[j, ks], peak_in.at[slot, ks], m_send.at[g, j], m_recv.at[g, slot], where),
        )

    def via(g):
        return hand(g, 0, jnp.where(inner, 3, 0), jnp.where(inner, opposite, near))

    def start(copies):
        for copy in copies:
            copy.start()

    def arrive(copies):
        for copy in copies:
            copy.wait_recv()

    both = (0, 1, 2)

    def give(g, j, slot, to):
        for k in groups[g]:
            encode(k, j, packed(k, to))
        return hand(g, j, slot, near if slot == 4 else to)

    def give_far(g):
        start(give(g, 2, 4 if g in both else 2, far))

    def give_via(g):
        for k in groups[g]:
            encode(k, 0, packed(k, opposite))
        start(via(g))

    def ready(g):
        if g in both:
            pl.when(jnp.logical_not(inner))(functools.partial(give_via, g))
        else:
            give_via(g)
        pl.when(jnp.logical_not(inner))(functools.partial(give_far, g))
        for k in groups[g]:
            total[k] = packed(k, lay)

    def send_near(g):
        start(give(g, 1, 1, near))

    def forward(g):
        @pl.when(inner)
        def _():
            arrive(hand(g, 0, 0, near))
            for k in groups[g]:
                encode(k, 2, packed(k, far) + decode(k, 0))
            start(hand(g, 2, 2, far))
            if g in both:
                arrive(hand(g, 0, 4, near))
                for k in groups[g]:
                    encode(k, 0, packed(k, opposite) + decode(k, 4))
                start(hand(g, 0, 3, opposite))

    def add(g, slot, to):
        arrive(hand(g, 0, slot, to))
        for k in groups[g]:
            total[k] += decode(k, slot)

    def collect(g):
        pl.when(inner)(functools.partial(add, g, 3, opposite))
        add(g, 1, near)
        if g in both:
            pl.when(jnp.logical_not(inner))(functools.partial(add, g, 2, far))
        else:
            add(g, 2, far)

    def fill(h):
        for d in range(1, chips):
            if h == 0:
                marks[d - 1].wait_recv()
            across[d, h].wait_recv()
            take_p(d, h)
        for d in range(1, n_col):
            if h == 0:
                over_marks[d].wait_recv()
            over[d, h].wait_recv()
            take_a(d, h)

    own_a.wait()
    take_p(0, 0)
    take_a(0, 0)
    take_p(0, 1)
    take_a(0, 1)
    fill(0)
    for d in range(chips):
        shared[d, 0].wait_recv()
    multiply(0, 0, pl.ds(0, 256))
    ready(0)
    send_near(0)
    fill(1)
    multiply(1, 0, pl.ds(256, 256))
    ready(1)
    pl.when(inner)(lambda: send_near(1))
    forward(0)
    for d in range(chips):
        shared[d, 1].wait_recv()
    multiply(2, 1, pl.ds(0, 512))
    ready(2)
    pl.when(jnp.logical_not(inner))(lambda: send_near(1))
    send_near(2)
    forward(1)
    forward(2)
    for g in range(3):
        collect(g)
    for rh in range(2):
        f, g = total[rh], total[2 + rh]
        for s in range(2):
            if s == 0:
                x = four(lane, [f, pltpu.roll(g, 32, 1), pltpu.roll(f, 32, 1), pltpu.roll(g, 64, 1)])
            else:
                x = four(lane, [pltpu.roll(f, 64, 1), pltpu.roll(g, 96, 1), pltpu.roll(f, 96, 1), g])
            out[pl.ds(rh * 32 + s * 16, 16)] = x.reshape(16, 8, LANES)

    sums = []
    for g in range(3):
        sums += list(via(g)) + list(hand(g, 2, 2, far)) + list(hand(g, 1, 1, near))
    for copy in list(across.values()) + list(shared.values()) + list(over.values()) + list(over_marks.values()):
        copy.wait_send()
    for copy in marks + sums:
        copy.wait_send()


def solution(mesh):
    n_row, n_col, n_layer = (mesh.shape[k] for k in ("row", "col", "layer"))

    def on_device(a_vals, a_rows, a_cols, a_count, p_vals, p_rows, p_cols, p_count):
        slots = a_vals.shape[3]
        wide = BS * BS
        any_space = pl.BlockSpec(memory_space=pltpu.HBM)
        vmem = pl.BlockSpec(memory_space=pltpu.VMEM)
        scalar = pl.BlockSpec(memory_space=pltpu.SMEM)

        def keep(x, shape):
            return pltpu.with_memory_space_constraint(x.reshape(shape), pltpu.HBM)

        dma = pltpu.SemaphoreType.DMA
        chips = n_row // 2
        got = pl.pallas_call(
            functools.partial(kernel, n_row, n_col, n_layer),
            out_shape=jax.ShapeDtypeStruct((BS, RB, LANES), F32),
            in_specs=[any_space] * 6 + [scalar] * 2,
            out_specs=vmem,
            scratch_shapes=(
                [pltpu.VMEM((1, slots), jnp.int32)] * 4
            ) + [
                pltpu.VMEM((n_col, slots, wide), BF16),
                pltpu.VMEM((slots, wide), BF16),
                pltpu.VMEM((chips, 2, slots, HALF), BF16),
                pltpu.VMEM((n_col, 8, LANES), jnp.int32),
                pltpu.VMEM((chips, 8, LANES), jnp.int32),
                pltpu.VMEM((8, LANES), jnp.int32),
                pltpu.VMEM((8, LANES), jnp.int32),
                pltpu.VMEM((n_row, RB * BS, 8 * BS), BF16),
                pltpu.VMEM((2, RB * BS, 8 * BS), BF16),
                pltpu.VMEM((2, n_row, 8 * BS, JB * BS // 2), BF16),
                pltpu.VMEM((8 * BS, 8 * BS), BF16),
                pltpu.VMEM((4, 256, 256), F32),
                pltpu.VMEM((4, LANES, LANES), F32),
                pltpu.VMEM((3, 4, LANES, LANES), jnp.int16),
                pltpu.VMEM((5, 4, LANES, LANES), jnp.int16),
                pltpu.VMEM((3, 4, 1, LANES), F32),
                pltpu.VMEM((5, 4, 1, LANES), F32),
                dma((8,)),
                dma((n_col, 2)), dma((n_col, 2)), dma((n_col,)), dma((n_col,)),
                dma((chips, 2)), dma((chips, 2)), dma((chips, 2)), dma((chips, 2)),
                dma((chips,)), dma((chips,)),
                dma((3, 3)), dma((3, 5)), dma((3, 3)), dma((3, 5)),
            ],
            compiler_params=pltpu.CompilerParams(
                collective_id=0, has_side_effects=True, vmem_limit_bytes=40 * 2**20
            ),
        )(
            keep(a_vals, (slots, wide)), keep(p_vals, (slots, wide)), keep(a_rows, (1, slots)), keep(a_cols, (1, slots)),
            keep(p_rows, (1, slots)), keep(p_cols, (1, slots)), a_count.reshape(1, 1), p_count.reshape(1, 1),
        )
        return got.transpose(1, 0, 2).reshape(RB * BS, LANES)

    placed = (
        P("row", "col", "layer", None, None),
        P("row", "col", "layer", None),
        P("row", "col", "layer", None),
        P("row", "col", "layer"),
    ) * 2
    return jax.shard_map(
        on_device, mesh=mesh, in_specs=placed, out_specs=P("row", ("col", "layer")), check_vma=False
    )
```

```python
import functools

import jax
import jax.numpy as jnp
from jax import lax
from jax.experimental import pallas as pl
from jax.experimental.pallas import tpu as pltpu
from jax.sharding import PartitionSpec as P

BS = 64
RB = 8
KB = 16
JB = 8
LANES = 128
HALF = BS * BS // 2
MESH = pl.DeviceIdType.MESH
F32 = jnp.float32
BF16 = jnp.bfloat16


def positions(rows, cols, count, width):
    slot = lax.broadcasted_iota(jnp.int32, rows.shape, 1)
    pos = jnp.where(slot < count, rows * width + cols, -1)
    row = jnp.concatenate([pos] * (LANES // pos.shape[1]), axis=1)
    return jnp.broadcast_to(row, (8, LANES))


def pair_onehot(pos, pairs, width, slots):
    shape = (pairs * 8, 2 * slots)
    row = lax.broadcasted_iota(jnp.int32, shape, 0)
    lane = lax.broadcasted_iota(jnp.int32, shape, 1)
    want = (row % 8) * width + 2 * (row // 8) + lane // slots
    return jnp.where(want == pos[0:1, : 2 * slots], 1.0, 0.0).astype(BF16)


def spread(vals, onehot, pairs, store, first=0, last=8):
    slots = vals.shape[0]
    low = lax.broadcasted_iota(jnp.int32, (slots, LANES), 1) < BS

    def body(step, carry):
        v = vals[:, pl.ds(pl.multiple_of(step * 512, 512), 512)].astype(F32)
        parts = []
        for g in range(4):
            a = v[:, g * LANES : (g + 1) * LANES]
            b = pltpu.roll(a, BS, 1)
            parts.append(jnp.concatenate([jnp.where(low, a, 0.0), jnp.where(low, 0.0, b)], axis=0))
            parts.append(jnp.concatenate([jnp.where(low, b, 0.0), jnp.where(low, 0.0, a)], axis=0))
        w = jnp.concatenate(parts, axis=1).astype(BF16)
        d = jnp.dot(onehot, w, preferred_element_type=F32)
        for p in range(pairs):
            rows = [d[p * 8 : (p + 1) * 8, i * LANES : (i + 1) * LANES] for i in range(8)]
            store(step, p, jnp.concatenate(rows, axis=0).astype(BF16))
        return carry

    lax.fori_loop(first, last, body, 0, unroll=True)


def quad_onehot(pos, slots):
    row = lax.broadcasted_iota(jnp.int32, (64, slots), 0)
    want = (row % 8) * JB + ((row // 8) % 2) * 4 + row // 16
    return jnp.where(want == pos[0:1, :slots], 1.0, 0.0).astype(BF16)


def lane_of(shape):
    return lax.broadcasted_iota(jnp.int32, shape, 1)


def four(lane, parts):
    low = jnp.where(lane < 32, parts[0], parts[1])
    high = jnp.where(lane < 96, parts[2], parts[3])
    return jnp.where(lane < 64, low, high)


def split(src, dst):
    slots = src.shape[0]
    first = lane_of((slots, LANES)) % BS < 32
    for t in range(16):
        a = src[:, 256 * t : 256 * t + LANES].astype(F32)
        b = src[:, 256 * t + LANES : 256 * t + 256].astype(F32)
        at = slice(t * LANES, (t + 1) * LANES)
        dst[0, :, at] = jnp.where(first, a, pltpu.roll(b, 32, 1)).astype(BF16)
        dst[1, :, at] = jnp.where(first, pltpu.roll(a, 96, 1), b).astype(BF16)


def spread_half(vals, onehot, store):
    lane = lane_of((8, LANES))
    for step in range(4):
        v = vals[:, step * 512 : (step + 1) * 512].astype(F32)
        parts = []
        for g in range(4):
            a = v[:, g * LANES : (g + 1) * LANES]
            parts += [a] + [pltpu.roll(a, 32 * r, 1) for r in range(1, 4)]
        w = jnp.concatenate(parts, axis=1).astype(BF16)
        d = jnp.dot(onehot, w, preferred_element_type=F32)
        for z in range(2):
            rows = []
            for kin in range(16):
                g, u = kin // 4, (0, 2, 1, 3)[kin % 4]
                at = [(g * 4 + (m - u) % 4) * LANES for m in range(4)]
                rows.append(
                    four(lane, [d[m * 16 + z * 8 : m * 16 + z * 8 + 8, at[m] : at[m] + LANES] for m in range(4)])
                )
            store(step, z, jnp.concatenate(rows, axis=0).astype(BF16))


def kernel(
    n_row, n_col, n_layer, a_hbm, p_hbm, *rest,
):
    small_hbm, (a_count, p_count), out, small, scratch = rest[:4], rest[4:6], rest[6], rest[7:11], rest[11:]
    (
    a_buf, p_raw, p_buf, a_pos, p_pos, a_own_pos, p_own_pos, a_dense, a_mixed, p_dense, order, acc, total,
    code, code_in, peak, peak_in,
    loc_sem, a_send, a_recv, ap_send, ap_recv, p_send, p_recv, r_send, r_recv, pp_send, pp_recv,
    c_send, c_recv, m_send, m_recv,
    ) = scratch
    row, col, lay = lax.axis_index("row"), lax.axis_index("col"), lax.axis_index("layer")
    core = lax.rem(row, 2)
    sib = row + 1 - 2 * core
    chips = n_row // 2
    slots = a_hbm.shape[0]

    barrier = pltpu.get_barrier_semaphore()
    for d in range(1, n_row):
        pl.semaphore_signal(barrier, inc=1, device_id={"row": lax.rem(row + d, n_row)}, device_id_type=MESH)
    for d in range(1, n_col):
        pl.semaphore_signal(barrier, inc=1, device_id={"col": lax.rem(col + d, n_col)}, device_id_type=MESH)
    for d in range(1, n_layer):
        pl.semaphore_signal(barrier, inc=1, device_id={"layer": lax.rem(lay + d, n_layer)}, device_id_type=MESH)
    own_a = pltpu.make_async_copy(a_hbm, a_buf.at[0], loc_sem.at[0])
    own_p = pltpu.make_async_copy(p_hbm, p_raw, loc_sem.at[1])
    tables = [pltpu.make_async_copy(small_hbm[k], small[k], loc_sem.at[2 + k]) for k in range(4)]
    own_p.start()
    for copy in tables:
        copy.start()
    own_a.start()

    def remote(src, dst, send, recv, where):
        return pltpu.make_async_remote_copy(
            src_ref=src, dst_ref=dst, send_sem=send, recv_sem=recv, device_id=where, device_id_type=MESH
        )

    def piece(ref, h):
        return ref.at[:, pl.ds(h * HALF, HALF)]

    across, shared, over, over_marks, marks = {}, {}, {}, {}, []
    for h in range(2):
        for d in range(chips):
            to = {"row": lax.rem(row + 2 * d, n_row)}
            if d:
                across[d, h] = remote(p_buf.at[0, h], p_buf.at[d, h], p_send.at[d, h], p_recv.at[d, h], to)
            mine, theirs = p_dense.at[h, 2 * d], p_dense.at[h, 2 * d + 1]
            shared[d, h] = remote(mine, theirs, r_send.at[d, h], r_recv.at[d, h], {"row": sib})
        for d in range(1, n_col):
            to = {"col": lax.rem(col + d, n_col)}
            over[d, h] = remote(piece(a_hbm, h), piece(a_buf.at[d], h), a_send.at[d, h], a_recv.at[d, h], to)
    for d in range(1, n_col):
        to = {"col": lax.rem(col + d, n_col)}
        over_marks[d] = remote(a_own_pos, a_pos.at[d], ap_send.at[d], ap_recv.at[d], to)
    for d in range(1, chips):
        to = {"row": lax.rem(row + 2 * d, n_row)}
        marks.append(remote(p_own_pos, p_pos.at[d], pp_send.at[d], pp_recv.at[d], to))

    own_p.wait()
    split(p_raw, p_buf.at[0])
    for copy in tables:
        copy.wait()
    a_rows, a_cols, p_rows, p_cols = small
    a_own_pos[...] = positions(a_rows[...], a_cols[...], a_count[0, 0], KB)
    p_own_pos[...] = positions(p_rows[...], p_cols[...], p_count[0, 0], JB)
    pl.semaphore_wait(barrier, n_row + n_col + n_layer - 3)
    for h in range(2):
        for d in range(1, chips):
            across[d, h].start()
        for d in range(1, n_col):
            over[d, h].start()
        if h == 0:
            for copy in marks + list(over_marks.values()):
                copy.start()

    shape = order.shape
    r = lax.broadcasted_iota(jnp.int32, shape, 0)
    c = lax.broadcasted_iota(jnp.int32, shape, 1)
    order[...] = jnp.where(c == (r % BS) * 8 + r // BS, 1.0, 0.0).astype(BF16)

    def take_a(d, h):
        pos = a_own_pos if d == 0 else a_pos.at[d]
        onehot = pair_onehot(pos[...], KB // 2, KB, slots)
        first = 2 * lax.rem(col - d + n_col, n_col)

        def store(step, p, rows):
            lanes = pl.ds((p % 4) * LANES, LANES)
            a_mixed[p // 4, pl.ds(pl.multiple_of(step * 64, 64), 64), lanes] = rows

        spread(a_buf.at[d], onehot, KB // 2, store, 4 * h, 4 * h + 4)
        rows = pl.ds(h * 256, 256)
        for q in range(2):
            a_dense[first + q, rows, :] = jnp.dot(
                a_mixed[q, rows, :], order[...], preferred_element_type=F32
            ).astype(BF16)

    def take_p(d, h):
        pos = p_own_pos if d == 0 else p_pos.at[d]

        def store(step, z, rows):
            p_dense[h, 2 * d, step * LANES : (step + 1) * LANES, z * LANES : (z + 1) * LANES] = rows

        spread_half(p_buf.at[d, h], quad_onehot(pos[...], slots), store)
        shared[d, h].start()

    def source(d):
        base = row if d % 2 == 0 else sib
        return lax.rem(base - 2 * (d // 2) + n_row, n_row)

    inner = jnp.logical_or(lay == 1, lay == 2)
    near = lay + 1 - 2 * lax.rem(lay, 2)
    far = lax.rem(lay + 2, 4)
    opposite = 3 - lay
    lane = lane_of((LANES, LANES))

    def multiply(first, ch, rows):
        total_ = jnp.dot(a_dense[source(0), rows, :], p_dense[ch, 0], preferred_element_type=F32)
        for d in range(1, n_row):
            total_ += jnp.dot(a_dense[source(d), rows, :], p_dense[ch, d], preferred_element_type=F32)
        for k in range(total_.shape[0] // 256):
            acc[first + k] = total_[k * 256 : (k + 1) * 256]

    def packed(k, to):
        lanes = pl.ds(pl.multiple_of((to // 2) * LANES, LANES), LANES)
        x, y = acc[k, 0:LANES, lanes], acc[k, LANES : 2 * LANES, lanes]
        odd = lax.rem(to, 2)
        stays = jnp.where(odd == 0, x, y)
        moves = pltpu.roll(jnp.where(odd == 0, y, x), BS, 1)
        return jnp.where(lane // BS == odd, stays, moves)

    def encode(k, j, x):
        top = jnp.maximum(jnp.max(jnp.abs(x), axis=0, keepdims=True), 1.2e-38)
        peak[j, k] = top
        q = jnp.round((x * (1.0 / top)) * 32767.0)
        code[j, k] = q.astype(jnp.int32).astype(jnp.int16)

    def decode(k, slot):
        q = code_in[slot, k].astype(jnp.int32).astype(F32)
        return (q * (1.0 / 32767.0)) * peak_in[slot, k]

    groups = ((0,), (1,), (2, 3))

    def hand(g, j, slot, to):
        where, ks = {"layer": to}, pl.ds(groups[g][0], len(groups[g]))
        return (
            remote(code.at[j, ks], code_in.at[slot, ks], c_send.at[g, j], c_recv.at[g, slot], where),
            remote(peak.at[j, ks], peak_in.at[slot, ks], m_send.at[g, j], m_recv.at[g, slot], where),
        )

    def via(g):
        return hand(g, 0, jnp.where(inner, 3, 0), jnp.where(inner, opposite, near))

    def start(copies):
        for copy in copies:
            copy.start()

    def arrive(copies):
        for copy in copies:
            copy.wait_recv()

    both = (0, 1, 2)

    def give(g, j, slot, to):
        for k in groups[g]:
            encode(k, j, packed(k, to))
        return hand(g, j, slot, near if slot == 4 else to)

    def give_far(g):
        start(give(g, 2, 4 if g in both else 2, far))

    def give_via(g):
        for k in groups[g]:
            encode(k, 0, packed(k, opposite))
        start(via(g))

    def ready(g):
        if g in both:
            pl.when(jnp.logical_not(inner))(functools.partial(give_via, g))
        else:
            give_via(g)
        pl.when(jnp.logical_not(inner))(functools.partial(give_far, g))
        for k in groups[g]:
            total[k] = packed(k, lay)

    def send_near(g):
        start(give(g, 1, 1, near))

    def forward(g):
        @pl.when(inner)
        def _():
            arrive(hand(g, 0, 0, near))
            for k in groups[g]:
                encode(k, 2, packed(k, far) + decode(k, 0))
            start(hand(g, 2, 2, far))
            if g in both:
                arrive(hand(g, 0, 4, near))
                for k in groups[g]:
                    encode(k, 0, packed(k, opposite) + decode(k, 4))
                start(hand(g, 0, 3, opposite))

    def add(g, slot, to):
        arrive(hand(g, 0, slot, to))
        for k in groups[g]:
            total[k] += decode(k, slot)

    def collect(g):
        pl.when(inner)(functools.partial(add, g, 3, opposite))
        add(g, 1, near)
        if g in both:
            pl.when(jnp.logical_not(inner))(functools.partial(add, g, 2, far))
        else:
            add(g, 2, far)

    def fill(h):
        for d in range(1, chips):
            if h == 0:
                marks[d - 1].wait_recv()
            across[d, h].wait_recv()
            take_p(d, h)
        for d in range(1, n_col):
            if h == 0:
                over_marks[d].wait_recv()
            over[d, h].wait_recv()
            take_a(d, h)

    own_a.wait()
    take_p(0, 0)
    take_a(0, 0)
    take_p(0, 1)
    take_a(0, 1)
    fill(0)
    for d in range(chips):
        shared[d, 0].wait_recv()
    multiply(0, 0, pl.ds(0, 256))
    ready(0)
    send_near(0)
    fill(1)
    multiply(1, 0, pl.ds(256, 256))
    ready(1)
    pl.when(inner)(lambda: send_near(1))
    for d in range(chips):
        shared[d, 1].wait_recv()
    forward(0)
    multiply(2, 1, pl.ds(0, 512))
    ready(2)
    pl.when(jnp.logical_not(inner))(lambda: send_near(1))
    send_near(2)
    forward(1)
    forward(2)
    for g in range(3):
        collect(g)
    for rh in range(2):
        f, g = total[rh], total[2 + rh]
        for s in range(2):
            if s == 0:
                x = four(lane, [f, pltpu.roll(g, 32, 1), pltpu.roll(f, 32, 1), pltpu.roll(g, 64, 1)])
            else:
                x = four(lane, [pltpu.roll(f, 64, 1), pltpu.roll(g, 96, 1), pltpu.roll(f, 96, 1), g])
            out[pl.ds(rh * 32 + s * 16, 16)] = x.reshape(16, 8, LANES)

    sums = []
    for g in range(3):
        sums += list(via(g)) + list(hand(g, 2, 2, far)) + list(hand(g, 1, 1, near))
    for copy in list(across.values()) + list(shared.values()) + list(over.values()) + list(over_marks.values()):
        copy.wait_send()
    for copy in marks + sums:
        copy.wait_send()


def solution(mesh):
    n_row, n_col, n_layer = (mesh.shape[k] for k in ("row", "col", "layer"))

    def on_device(a_vals, a_rows, a_cols, a_count, p_vals, p_rows, p_cols, p_count):
        slots = a_vals.shape[3]
        wide = BS * BS
        any_space = pl.BlockSpec(memory_space=pltpu.HBM)
        vmem = pl.BlockSpec(memory_space=pltpu.VMEM)
        scalar = pl.BlockSpec(memory_space=pltpu.SMEM)

        def keep(x, shape):
            return pltpu.with_memory_space_constraint(x.reshape(shape), pltpu.HBM)

        dma = pltpu.SemaphoreType.DMA
        chips = n_row // 2
        got = pl.pallas_call(
            functools.partial(kernel, n_row, n_col, n_layer),
            out_shape=jax.ShapeDtypeStruct((BS, RB, LANES), F32),
            in_specs=[any_space] * 6 + [scalar] * 2,
            out_specs=vmem,
            scratch_shapes=(
                [pltpu.VMEM((1, slots), jnp.int32)] * 4
            ) + [
                pltpu.VMEM((n_col, slots, wide), BF16),
                pltpu.VMEM((slots, wide), BF16),
                pltpu.VMEM((chips, 2, slots, HALF), BF16),
                pltpu.VMEM((n_col, 8, LANES), jnp.int32),
                pltpu.VMEM((chips, 8, LANES), jnp.int32),
                pltpu.VMEM((8, LANES), jnp.int32),
                pltpu.VMEM((8, LANES), jnp.int32),
                pltpu.VMEM((n_row, RB * BS, 8 * BS), BF16),
                pltpu.VMEM((2, RB * BS, 8 * BS), BF16),
                pltpu.VMEM((2, n_row, 8 * BS, JB * BS // 2), BF16),
                pltpu.VMEM((8 * BS, 8 * BS), BF16),
                pltpu.VMEM((4, 256, 256), F32),
                pltpu.VMEM((4, LANES, LANES), F32),
                pltpu.VMEM((3, 4, LANES, LANES), jnp.int16),
                pltpu.VMEM((5, 4, LANES, LANES), jnp.int16),
                pltpu.VMEM((3, 4, 1, LANES), F32),
                pltpu.VMEM((5, 4, 1, LANES), F32),
                dma((8,)),
                dma((n_col, 2)), dma((n_col, 2)), dma((n_col,)), dma((n_col,)),
                dma((chips, 2)), dma((chips, 2)), dma((chips, 2)), dma((chips, 2)),
                dma((chips,)), dma((chips,)),
                dma((3, 3)), dma((3, 5)), dma((3, 3)), dma((3, 5)),
            ],
            compiler_params=pltpu.CompilerParams(
                collective_id=0, has_side_effects=True, vmem_limit_bytes=40 * 2**20
            ),
        )(
            keep(a_vals, (slots, wide)), keep(p_vals, (slots, wide)), keep(a_rows, (1, slots)), keep(a_cols, (1, slots)),
            keep(p_rows, (1, slots)), keep(p_cols, (1, slots)), a_count.reshape(1, 1), p_count.reshape(1, 1),
        )
        return got.transpose(1, 0, 2).reshape(RB * BS, LANES)

    placed = (
        P("row", "col", "layer", None, None),
        P("row", "col", "layer", None),
        P("row", "col", "layer", None),
        P("row", "col", "layer"),
    ) * 2
    return jax.shard_map(
        on_device, mesh=mesh, in_specs=placed, out_specs=P("row", ("col", "layer")), check_vma=False
    )
```

```python
import functools

import jax
import jax.numpy as jnp
from jax import lax
from jax.experimental import pallas as pl
from jax.experimental.pallas import tpu as pltpu
from jax.sharding import PartitionSpec as P

BS = 64
RB = 8
KB = 16
JB = 8
LANES = 128
HALF = BS * BS // 2
MESH = pl.DeviceIdType.MESH
F32 = jnp.float32
BF16 = jnp.bfloat16


def positions(rows, cols, count, width):
    slot = lax.broadcasted_iota(jnp.int32, rows.shape, 1)
    pos = jnp.where(slot < count, rows * width + cols, -1)
    row = jnp.concatenate([pos] * (LANES // pos.shape[1]), axis=1)
    return jnp.broadcast_to(row, (8, LANES))


def pair_onehot(pos, pairs, width, slots):
    shape = (pairs * 8, 2 * slots)
    row = lax.broadcasted_iota(jnp.int32, shape, 0)
    lane = lax.broadcasted_iota(jnp.int32, shape, 1)
    want = (row % 8) * width + 2 * (row // 8) + lane // slots
    return jnp.where(want == pos[0:1, : 2 * slots], 1.0, 0.0).astype(BF16)


def spread(vals, onehot, pairs, store, first=0, last=8):
    slots = vals.shape[0]
    low = lax.broadcasted_iota(jnp.int32, (slots, LANES), 1) < BS

    def body(step, carry):
        v = vals[:, pl.ds(pl.multiple_of(step * 512, 512), 512)].astype(F32)
        parts = []
        for g in range(4):
            a = v[:, g * LANES : (g + 1) * LANES]
            b = pltpu.roll(a, BS, 1)
            parts.append(jnp.concatenate([jnp.where(low, a, 0.0), jnp.where(low, 0.0, b)], axis=0))
            parts.append(jnp.concatenate([jnp.where(low, b, 0.0), jnp.where(low, 0.0, a)], axis=0))
        w = jnp.concatenate(parts, axis=1).astype(BF16)
        d = jnp.dot(onehot, w, preferred_element_type=F32)
        for p in range(pairs):
            rows = [d[p * 8 : (p + 1) * 8, i * LANES : (i + 1) * LANES] for i in range(8)]
            store(step, p, jnp.concatenate(rows, axis=0).astype(BF16))
        return carry

    lax.fori_loop(first, last, body, 0, unroll=True)


def quad_onehot(pos, slots):
    row = lax.broadcasted_iota(jnp.int32, (64, slots), 0)
    want = (row % 8) * JB + ((row // 8) % 2) * 4 + row // 16
    return jnp.where(want == pos[0:1, :slots], 1.0, 0.0).astype(BF16)


def lane_of(shape):
    return lax.broadcasted_iota(jnp.int32, shape, 1)


def four(lane, parts):
    low = jnp.where(lane < 32, parts[0], parts[1])
    high = jnp.where(lane < 96, parts[2], parts[3])
    return jnp.where(lane < 64, low, high)


def split(src, dst):
    slots = src.shape[0]
    first = lane_of((slots, LANES)) % BS < 32
    for t in range(16):
        a = src[:, 256 * t : 256 * t + LANES].astype(F32)
        b = src[:, 256 * t + LANES : 256 * t + 256].astype(F32)
        at = slice(t * LANES, (t + 1) * LANES)
        dst[0, :, at] = jnp.where(first, a, pltpu.roll(b, 32, 1)).astype(BF16)
        dst[1, :, at] = jnp.where(first, pltpu.roll(a, 96, 1), b).astype(BF16)


def spread_half(vals, onehot, store):
    lane = lane_of((8, LANES))
    for step in range(4):
        v = vals[:, step * 512 : (step + 1) * 512].astype(F32)
        parts = []
        for g in range(4):
            a = v[:, g * LANES : (g + 1) * LANES]
            parts += [a] + [pltpu.roll(a, 32 * r, 1) for r in range(1, 4)]
        w = jnp.concatenate(parts, axis=1).astype(BF16)
        d = jnp.dot(onehot, w, preferred_element_type=F32)
        for z in range(2):
            rows = []
            for kin in range(16):
                g, u = kin // 4, (0, 2, 1, 3)[kin % 4]
                at = [(g * 4 + (m - u) % 4) * LANES for m in range(4)]
                rows.append(
                    four(lane, [d[m * 16 + z * 8 : m * 16 + z * 8 + 8, at[m] : at[m] + LANES] for m in range(4)])
                )
            store(step, z, jnp.concatenate(rows, axis=0).astype(BF16))


def kernel(
    n_row, n_col, n_layer, a_hbm, p_hbm, *rest,
):
    small_hbm, (a_count, p_count), out, small, scratch = rest[:4], rest[4:6], rest[6], rest[7:11], rest[11:]
    (
    a_buf, p_raw, p_buf, a_pos, p_pos, a_own_pos, p_own_pos, a_dense, a_mixed, p_dense, order, acc, total,
    code, code_in, peak, peak_in,
    loc_sem, a_send, a_recv, ap_send, ap_recv, p_send, p_recv, r_send, r_recv, pp_send, pp_recv,
    c_send, c_recv, m_send, m_recv,
    ) = scratch
    row, col, lay = lax.axis_index("row"), lax.axis_index("col"), lax.axis_index("layer")
    core = lax.rem(row, 2)
    sib = row + 1 - 2 * core
    chips = n_row // 2
    slots = a_hbm.shape[0]

    barrier = pltpu.get_barrier_semaphore()
    for d in range(1, n_row):
        pl.semaphore_signal(barrier, inc=1, device_id={"row": lax.rem(row + d, n_row)}, device_id_type=MESH)
    for d in range(1, n_col):
        pl.semaphore_signal(barrier, inc=1, device_id={"col": lax.rem(col + d, n_col)}, device_id_type=MESH)
    for d in range(1, n_layer):
        pl.semaphore_signal(barrier, inc=1, device_id={"layer": lax.rem(lay + d, n_layer)}, device_id_type=MESH)
    own_a = pltpu.make_async_copy(a_hbm, a_buf.at[0], loc_sem.at[0])
    own_p = pltpu.make_async_copy(p_hbm, p_raw, loc_sem.at[1])
    tables = [pltpu.make_async_copy(small_hbm[k], small[k], loc_sem.at[2 + k]) for k in range(4)]
    own_p.start()
    for copy in tables:
        copy.start()
    own_a.start()

    def remote(src, dst, send, recv, where):
        return pltpu.make_async_remote_copy(
            src_ref=src, dst_ref=dst, send_sem=send, recv_sem=recv, device_id=where, device_id_type=MESH
        )

    def piece(ref, h):
        return ref.at[:, pl.ds(h * HALF, HALF)]

    across, shared, over, over_marks, marks = {}, {}, {}, {}, []
    for h in range(2):
        for d in range(chips):
            to = {"row": lax.rem(row + 2 * d, n_row)}
            if d:
                across[d, h] = remote(p_buf.at[0, h], p_buf.at[d, h], p_send.at[d, h], p_recv.at[d, h], to)
            mine, theirs = p_dense.at[h, 2 * d], p_dense.at[h, 2 * d + 1]
            shared[d, h] = remote(mine, theirs, r_send.at[d, h], r_recv.at[d, h], {"row": sib})
        for d in range(1, n_col):
            to = {"col": lax.rem(col + d, n_col)}
            over[d, h] = remote(piece(a_hbm, h), piece(a_buf.at[d], h), a_send.at[d, h], a_recv.at[d, h], to)
    for d in range(1, n_col):
        to = {"col": lax.rem(col + d, n_col)}
        over_marks[d] = remote(a_own_pos, a_pos.at[d], ap_send.at[d], ap_recv.at[d], to)
    for d in range(1, chips):
        to = {"row": lax.rem(row + 2 * d, n_row)}
        marks.append(remote(p_own_pos, p_pos.at[d], pp_send.at[d], pp_recv.at[d], to))

    own_p.wait()
    split(p_raw, p_buf.at[0])
    for copy in tables:
        copy.wait()
    a_rows, a_cols, p_rows, p_cols = small
    a_own_pos[...] = positions(a_rows[...], a_cols[...], a_count[0, 0], KB)
    p_own_pos[...] = positions(p_rows[...], p_cols[...], p_count[0, 0], JB)
    pl.semaphore_wait(barrier, n_row + n_col + n_layer - 3)
    for h in range(2):
        for d in range(1, chips):
            across[d, h].start()
        for d in range(1, n_col):
            over[d, h].start()
        if h == 0:
            for copy in marks + list(over_marks.values()):
                copy.start()

    shape = order.shape
    r = lax.broadcasted_iota(jnp.int32, shape, 0)
    c = lax.broadcasted_iota(jnp.int32, shape, 1)
    order[...] = jnp.where(c == (r % BS) * 8 + r // BS, 1.0, 0.0).astype(BF16)

    def take_a(d, h):
        pos = a_own_pos if d == 0 else a_pos.at[d]
        onehot = pair_onehot(pos[...], KB // 2, KB, slots)
        first = 2 * lax.rem(col - d + n_col, n_col)

        def store(step, p, rows):
            lanes = pl.ds((p % 4) * LANES, LANES)
            a_mixed[p // 4, pl.ds(pl.multiple_of(step * 64, 64), 64), lanes] = rows

        spread(a_buf.at[d], onehot, KB // 2, store, 4 * h, 4 * h + 4)
        rows = pl.ds(h * 256, 256)
        for q in range(2):
            a_dense[first + q, rows, :] = jnp.dot(
                a_mixed[q, rows, :], order[...], preferred_element_type=F32
            ).astype(BF16)

    def take_p(d, h):
        pos = p_own_pos if d == 0 else p_pos.at[d]

        def store(step, z, rows):
            p_dense[h, 2 * d, step * LANES : (step + 1) * LANES, z * LANES : (z + 1) * LANES] = rows

        spread_half(p_buf.at[d, h], quad_onehot(pos[...], slots), store)
        shared[d, h].start()

    def source(d):
        base = row if d % 2 == 0 else sib
        return lax.rem(base - 2 * (d // 2) + n_row, n_row)

    inner = jnp.logical_or(lay == 1, lay == 2)
    near = lay + 1 - 2 * lax.rem(lay, 2)
    far = lax.rem(lay + 2, 4)
    opposite = 3 - lay
    lane = lane_of((LANES, LANES))

    def multiply(first, ch, rows):
        total_ = jnp.dot(a_dense[source(0), rows, :], p_dense[ch, 0], preferred_element_type=F32)
        for d in range(1, n_row):
            total_ += jnp.dot(a_dense[source(d), rows, :], p_dense[ch, d], preferred_element_type=F32)
        for k in range(total_.shape[0] // 256):
            acc[first + k] = total_[k * 256 : (k + 1) * 256]

    def packed(k, to):
        lanes = pl.ds(pl.multiple_of((to // 2) * LANES, LANES), LANES)
        x, y = acc[k, 0:LANES, lanes], acc[k, LANES : 2 * LANES, lanes]
        odd = lax.rem(to, 2)
        stays = jnp.where(odd == 0, x, y)
        moves = pltpu.roll(jnp.where(odd == 0, y, x), BS, 1)
        return jnp.where(lane // BS == odd, stays, moves)

    def encode(k, j, x):
        top = jnp.maximum(jnp.max(jnp.abs(x), axis=0, keepdims=True), 1.2e-38)
        peak[j, k] = top
        q = jnp.round((x * (1.0 / top)) * 32767.0)
        code[j, k] = q.astype(jnp.int32).astype(jnp.int16)

    def decode(k, slot):
        q = code_in[slot, k].astype(jnp.int32).astype(F32)
        return (q * (1.0 / 32767.0)) * peak_in[slot, k]

    groups = ((0,), (1,), (2, 3))

    def hand(g, j, slot, to):
        where, ks = {"layer": to}, pl.ds(groups[g][0], len(groups[g]))
        return (
            remote(code.at[j, ks], code_in.at[slot, ks], c_send.at[g, j], c_recv.at[g, slot], where),
            remote(peak.at[j, ks], peak_in.at[slot, ks], m_send.at[g, j], m_recv.at[g, slot], where),
        )

    def via(g):
        return hand(g, 0, jnp.where(inner, 3, 0), jnp.where(inner, opposite, near))

    def start(copies):
        for copy in copies:
            copy.start()

    def arrive(copies):
        for copy in copies:
            copy.wait_recv()

    both = (0, 1, 2)

    def give(g, j, slot, to):
        for k in groups[g]:
            encode(k, j, packed(k, to))
        return hand(g, j, slot, near if slot == 4 else to)

    def give_far(g):
        start(give(g, 2, 4 if g in both else 2, far))

    def give_via(g):
        for k in groups[g]:
            encode(k, 0, packed(k, opposite))
        start(via(g))

    def ready(g):
        if g in both:
            pl.when(jnp.logical_not(inner))(functools.partial(give_via, g))
        else:
            give_via(g)
        pl.when(jnp.logical_not(inner))(functools.partial(give_far, g))
        for k in groups[g]:
            total[k] = packed(k, lay)

    def send_near(g):
        start(give(g, 1, 1, near))

    def forward(g):
        @pl.when(inner)
        def _():
            arrive(hand(g, 0, 0, near))
            for k in groups[g]:
                encode(k, 2, packed(k, far) + decode(k, 0))
            start(hand(g, 2, 2, far))
            if g in both:
                arrive(hand(g, 0, 4, near))
                for k in groups[g]:
                    encode(k, 0, packed(k, opposite) + decode(k, 4))
                start(hand(g, 0, 3, opposite))

    def add(g, slot, to):
        arrive(hand(g, 0, slot, to))
        for k in groups[g]:
            total[k] += decode(k, slot)

    def collect(g):
        pl.when(inner)(functools.partial(add, g, 3, opposite))
        add(g, 1, near)
        if g in both:
            pl.when(jnp.logical_not(inner))(functools.partial(add, g, 2, far))
        else:
            add(g, 2, far)

    def fill(h):
        for d in range(1, chips):
            if h == 0:
                marks[d - 1].wait_recv()
            across[d, h].wait_recv()
            take_p(d, h)
        for d in range(1, n_col):
            if h == 0:
                over_marks[d].wait_recv()
            over[d, h].wait_recv()
            take_a(d, h)

    own_a.wait()
    take_p(0, 0)
    take_a(0, 0)
    take_p(0, 1)
    take_a(0, 1)
    fill(0)
    for d in range(chips):
        shared[d, 0].wait_recv()
    multiply(0, 0, pl.ds(0, 256))
    ready(0)
    send_near(0)
    fill(1)
    multiply(1, 0, pl.ds(256, 256))
    ready(1)
    pl.when(inner)(lambda: send_near(1))
    for d in range(chips):
        shared[d, 1].wait_recv()
    multiply(2, 1, pl.ds(0, 512))
    ready(2)
    forward(0)
    pl.when(jnp.logical_not(inner))(lambda: send_near(1))
    send_near(2)
    forward(1)
    forward(2)
    for g in range(3):
        collect(g)
    for rh in range(2):
        f, g = total[rh], total[2 + rh]
        for s in range(2):
            if s == 0:
                x = four(lane, [f, pltpu.roll(g, 32, 1), pltpu.roll(f, 32, 1), pltpu.roll(g, 64, 1)])
            else:
                x = four(lane, [pltpu.roll(f, 64, 1), pltpu.roll(g, 96, 1), pltpu.roll(f, 96, 1), g])
            out[pl.ds(rh * 32 + s * 16, 16)] = x.reshape(16, 8, LANES)

    sums = []
    for g in range(3):
        sums += list(via(g)) + list(hand(g, 2, 2, far)) + list(hand(g, 1, 1, near))
    for copy in list(across.values()) + list(shared.values()) + list(over.values()) + list(over_marks.values()):
        copy.wait_send()
    for copy in marks + sums:
        copy.wait_send()


def solution(mesh):
    n_row, n_col, n_layer = (mesh.shape[k] for k in ("row", "col", "layer"))

    def on_device(a_vals, a_rows, a_cols, a_count, p_vals, p_rows, p_cols, p_count):
        slots = a_vals.shape[3]
        wide = BS * BS
        any_space = pl.BlockSpec(memory_space=pltpu.HBM)
        vmem = pl.BlockSpec(memory_space=pltpu.VMEM)
        scalar = pl.BlockSpec(memory_space=pltpu.SMEM)

        def keep(x, shape):
            return pltpu.with_memory_space_constraint(x.reshape(shape), pltpu.HBM)

        dma = pltpu.SemaphoreType.DMA
        chips = n_row // 2
        got = pl.pallas_call(
            functools.partial(kernel, n_row, n_col, n_layer),
            out_shape=jax.ShapeDtypeStruct((BS, RB, LANES), F32),
            in_specs=[any_space] * 6 + [scalar] * 2,
            out_specs=vmem,
            scratch_shapes=(
                [pltpu.VMEM((1, slots), jnp.int32)] * 4
            ) + [
                pltpu.VMEM((n_col, slots, wide), BF16),
                pltpu.VMEM((slots, wide), BF16),
                pltpu.VMEM((chips, 2, slots, HALF), BF16),
                pltpu.VMEM((n_col, 8, LANES), jnp.int32),
                pltpu.VMEM((chips, 8, LANES), jnp.int32),
                pltpu.VMEM((8, LANES), jnp.int32),
                pltpu.VMEM((8, LANES), jnp.int32),
                pltpu.VMEM((n_row, RB * BS, 8 * BS), BF16),
                pltpu.VMEM((2, RB * BS, 8 * BS), BF16),
                pltpu.VMEM((2, n_row, 8 * BS, JB * BS // 2), BF16),
                pltpu.VMEM((8 * BS, 8 * BS), BF16),
                pltpu.VMEM((4, 256, 256), F32),
                pltpu.VMEM((4, LANES, LANES), F32),
                pltpu.VMEM((3, 4, LANES, LANES), jnp.int16),
                pltpu.VMEM((5, 4, LANES, LANES), jnp.int16),
                pltpu.VMEM((3, 4, 1, LANES), F32),
                pltpu.VMEM((5, 4, 1, LANES), F32),
                dma((8,)),
                dma((n_col, 2)), dma((n_col, 2)), dma((n_col,)), dma((n_col,)),
                dma((chips, 2)), dma((chips, 2)), dma((chips, 2)), dma((chips, 2)),
                dma((chips,)), dma((chips,)),
                dma((3, 3)), dma((3, 5)), dma((3, 3)), dma((3, 5)),
            ],
            compiler_params=pltpu.CompilerParams(
                collective_id=0, has_side_effects=True, vmem_limit_bytes=40 * 2**20
            ),
        )(
            keep(a_vals, (slots, wide)), keep(p_vals, (slots, wide)), keep(a_rows, (1, slots)), keep(a_cols, (1, slots)),
            keep(p_rows, (1, slots)), keep(p_cols, (1, slots)), a_count.reshape(1, 1), p_count.reshape(1, 1),
        )
        return got.transpose(1, 0, 2).reshape(RB * BS, LANES)

    placed = (
        P("row", "col", "layer", None, None),
        P("row", "col", "layer", None),
        P("row", "col", "layer", None),
        P("row", "col", "layer"),
    ) * 2
    return jax.shard_map(
        on_device, mesh=mesh, in_specs=placed, out_specs=P("row", ("col", "layer")), check_vma=False
    )
```
